32 devices in a mesh: enc: 4 (over z), lab: 8 (over y, x, core).
Axes of the slice: x: 2, y: 2, z: 4, core: 2. Of those that a mesh axis runs over, the one named last changes fastest.
Arguments:
- embeddings: bfloat16 [16384, 768], P(('enc', 'lab')), may hold values from -6 to 6
- classifier: float32 [512, 768], P('lab'), may hold values from -0.21875 to 0.21875
- label_valid: int32 [512], P('lab'), may hold values 0 or 1
- shortlist: int32 [16384, 4], P(('enc', 'lab')), may hold values from 0 to 7, all different within a row; in each aligned block of 512 rows (0 to 511, 512 to 1023, ...) at most 384 rows name the same one
- slot_live: int32 [16384, 4], P(('enc', 'lab')), may hold values 0 or 1
- positive: int32 [16384, 4], P(('enc', 'lab')), may hold values from 0 to 63
- negative: int32 [16384, 4, 8], P(('enc', 'lab')), may hold values from 0 to 63
Outputs:
- w_grad: float32 [512, 768], P('lab')
- emb_grad: float32 [16384, 768], P(('enc', 'lab'))
The draws below stay inside these ranges and needn't reach their ends.
Inputs may be any that keep to these rules, and one draw needn't show every extreme that they name: `shortlist`: each document names 4 different clusters; among the 512 documents of one device no cluster is named by more than 384 documents.
All inputs are finite; a program needn't handle non-finite values. No bound on the sum of `label_valid` or of `slot_live` on one device may be relied on, other than what follows from the above.
Results may differ from the reference program's by a relative error of at most 0.0041.
Values may be sent and summed in bfloat16 or wider, within the bound.
No kernel may reach another device: no remote copies, remote signals or barrier semaphores. Data moves between devices by JAX's collectives and lax.ppermute only.
A program may use at most 128 MiB of HBM per device.

```python
import math
import jax
import jax.numpy as jnp
import numpy as np
from jax import lax

D = 768
PANEL = 64
S = 4
NNEG = 8
DOC_DEV = 512
CLUSTERS = 8
LABELS = 512
DOCS = 16384
CAP = 384
ROUTED = 8192


def set_ends(entries, stream_key, least, largest):
    longest = entries.shape.index(max(entries.shape))
    spots = []
    for shift in (0, 1):
        where = [jax.random.randint(jax.random.fold_in(stream_key, axis), (), 0, length) for axis, length in enumerate(entries.shape)]
        where[longest] = (where[longest] + shift) % entries.shape[longest]
        spots.append(tuple(where))
    return entries.at[spots[0]].set(least).at[spots[1]].set(largest)


def level_of(rng, dims, shards, low, top_value):
    factor_of = 1.0
    for dim, blocks in shards:
        heights = jax.random.uniform(jax.random.fold_in(jax.random.fold_in(rng, 6), dim), (blocks,), jnp.float32, low / len(shards), top_value / len(shards))
        factor_of = factor_of * jnp.repeat(jnp.exp(heights), dims[dim] // blocks).reshape((-1,) + (1,) * (len(dims) - 1 - dim))
    return factor_of


def deal_out(own_key, own, number, rows, amount, top, reach, slope):
    order = jax.random.permutation(own_key, amount)
    crowded, usual = load_shares(amount, rows * top, reach, slope, True), load_shares(amount, rows * top, reach, slope, False)
    places = jnp.arange(amount)

    def named(sizes, offset_by):
        used = int((sizes > 0).sum())
        fixed = max(1, used // 4)
        moved = fixed + (places - fixed + offset_by * (used - fixed)) % max(1, amount - fixed)
        return jnp.zeros((amount,), jnp.int32).at[order[jnp.where(places < fixed, places, moved)]].set(jnp.asarray(sizes, jnp.int32))

    sizes = jnp.where(number % 4 == 0, named(crowded, number // 4), named(usual, number - number // 4 - 1))
    mixed = jax.random.permutation(jax.random.fold_in(own, 3), amount)
    source_of, receiver = mixed[0:amount // 2 * 2:2], mixed[1:amount // 2 * 2:2]
    room = jnp.minimum(sizes[source_of] - 1, reach - sizes[receiver]) // 2
    room = jnp.where((source_of == order[0]) | (receiver == order[0]) | (sizes[receiver] == 0), 0, jnp.maximum(room, 0))
    moved = jax.random.randint(jax.random.fold_in(own, 4), (amount // 2,), 0, 1 << 20) % (room + 1)
    sizes = sizes.at[source_of].add(-moved).at[receiver].add(moved)
    members = jnp.searchsorted(jnp.cumsum(sizes), jnp.arange(rows * top), side="right").astype(jnp.int32)
    table = members.reshape(top, rows).T
    table = table[jax.random.permutation(jax.random.fold_in(own, 1), rows)]
    offset_by = jax.random.randint(jax.random.fold_in(own, 2), (rows, 1), 0, top)
    return jnp.take_along_axis(table, (jnp.arange(top)[None, :] + offset_by) % top, axis=1)


def load_shares(number_of, total, reach, skew, full):
    weights = [(1 << 20) // math.isqrt(rank ** skew) + 1 for rank in range(1, number_of + 1)]
    largest = reach if full else min(reach, max(-(-total // number_of), total * weights[0] // sum(weights)))
    least = 1 if total - largest >= number_of - 1 else 0
    holding, rest = [largest] + [least] * (number_of - 1), total - largest - least * (number_of - 1)
    while rest > 0:
        movable = [i for i in range(1, number_of) if holding[i] < largest] or [i for i in range(1, number_of) if holding[i] < reach]
        mass, remaining = sum([weights[i] for i in movable]), rest
        for i in movable:
            addition = min(reach - holding[i], max(1, remaining * weights[i] // mass), rest)
            holding[i] = holding[i] + addition
            rest = rest - addition
    return np.array(holding)


def scatter_about(rng, extent, width, reach, cuts=(), kind=jnp.bfloat16):
    result = width * jax.random.normal(rng, extent, jnp.float32)
    if cuts:
        result = result * level_of(rng, extent, cuts, -0.22, 0.18)
    return jnp.clip(result, -reach, reach).astype(kind)


def setup_inputs(seed: int = 0) -> dict:
    splits = jax.random.split(jax.random.key(seed), 8)
    embeddings = scatter_about(splits[0], (DOCS, D), 1.0, 6.0, ((0, 32),))
    classifier = scatter_about(splits[1], (LABELS, D), D ** -0.5, 0.21875, ((0, 8),), jnp.float32)
    label_valid = set_ends((jax.random.randint(splits[2], (LABELS,), 0, 16) < 15).astype(jnp.int32), jax.random.fold_in(splits[2], 1), 0, 1)
    shortlist_keys = jax.random.split(jax.random.fold_in(splits[3], 1), DOCS // DOC_DEV)
    shortlist_turns = jax.random.permutation(jax.random.fold_in(splits[3], 3), DOCS // DOC_DEV)
    shortlist = jax.vmap(lambda own, number: deal_out(jax.random.fold_in(splits[3], 2), own, number, DOC_DEV, CLUSTERS, S, CAP, 2))(shortlist_keys, shortlist_turns).reshape((DOCS, S))
    slot_live = set_ends((jax.random.randint(splits[4], (DOCS, S), 0, 8) < 7).astype(jnp.int32), jax.random.fold_in(splits[4], 1), 0, 1)
    positive = set_ends(jax.random.randint(splits[5], (DOCS, S), 0, PANEL), jax.random.fold_in(splits[5], 1), 0, PANEL - 1).astype(jnp.int32)
    negative = set_ends(jax.random.randint(splits[6], (DOCS, S, NNEG), 0, PANEL), jax.random.fold_in(splits[6], 1), 0, PANEL - 1).astype(jnp.int32)
    return {"embeddings": embeddings, "classifier": classifier, "label_valid": label_valid, "shortlist": shortlist, "slot_live": slot_live, "positive": positive, "negative": negative}


def dense_targets(shortlist, slot_live, positive, negative):
    labels = jnp.arange(PANEL, dtype=jnp.int32)
    pos_hot = (positive[..., None] == labels).astype(jnp.float32)
    neg_count = lax.optimization_barrier(jnp.sum((negative[..., None] == labels).astype(jnp.float32), axis=2))
    live = slot_live.astype(jnp.float32)[..., None]
    slot_weight = live * (pos_hot + neg_count)
    cluster_hot = (shortlist[..., None] == jnp.arange(CLUSTERS, dtype=jnp.int32)).astype(jnp.float32)
    count = shortlist.shape[0]
    weight = jnp.einsum('nsc,nsj->ncj', cluster_hot, slot_weight).reshape(count, LABELS)
    target = jnp.einsum('nsc,nsj->ncj', cluster_hot, pos_hot).reshape(count, LABELS)
    return (weight, target)

def reference(embeddings, classifier, label_valid, shortlist, slot_live, positive, negative):
    classifier_b = classifier.astype(jnp.bfloat16)
    valid = label_valid.astype(jnp.float32)
    blocks = DOCS // DOC_DEV
    emb_blocks = embeddings.reshape(blocks, DOC_DEV, D)
    short_blocks = shortlist.reshape(blocks, DOC_DEV, S)
    live_blocks = slot_live.reshape(blocks, DOC_DEV, S)
    pos_blocks = positive.reshape(blocks, DOC_DEV, S)
    neg_blocks = negative.reshape(blocks, DOC_DEV, S, NNEG)

    def one_block(total, inputs):
        emb_b, short_b, live_b, pos_b, neg_b = inputs
        weight, target = dense_targets(short_b, live_b, pos_b, neg_b)
        weight = weight * valid[None, :]
        logits = lax.dot_general(emb_b, classifier_b, (((1,), (1,)), ((), ())), preferred_element_type=jnp.float32)
        dlogits = (weight * (jax.nn.sigmoid(logits) - target)).astype(jnp.bfloat16)
        emb_grad = jnp.dot(dlogits, classifier_b, preferred_element_type=jnp.float32)
        total = total + lax.dot_general(dlogits, emb_b, (((0,), (0,)), ((), ())), preferred_element_type=jnp.float32)
        return (total, emb_grad)
    start = jnp.zeros((LABELS, D), jnp.float32)
    total, emb_grads = lax.scan(one_block, start, (emb_blocks, short_blocks, live_blocks, pos_blocks, neg_blocks))
    w_grad = total * (1.0 / math.sqrt(ROUTED))
    return (w_grad, emb_grads.reshape(DOCS, D))
```

```python
import functools
import math

import jax
import jax.numpy as jnp
from jax import lax
from jax.experimental import pallas as pl
from jax.experimental.pallas import tpu as pltpu
from jax.sharding import PartitionSpec as P

BF16 = jnp.bfloat16
F32 = jnp.float32
LANES = 128
SUBLANES = 8
ROWS = 256
VMEM_LIMIT = 56 * 1024 * 1024


def flip(value, axis, mask):
    return lax.ppermute(value, axis, [(i, i ^ mask) for i in range(lax.axis_size(axis))])


def bit_groups(count):
    masks = [1 << b for b in range(1, count.bit_length() - 1)]
    return [tuple(masks[i : i + 2]) for i in range(0, len(masks), 2)]


def group_masks(group):
    return [group[0]] if len(group) == 1 else [group[0], group[1], group[0] | group[1]]


def targets_kernel(short_ref, live_ref, pos_ref, neg_ref, mine_ref, theirs_ref, *, panel):
    me = lax.axis_index("lab")
    slots, docs = short_ref.shape
    negatives = neg_ref.shape[1]
    groups = panel // SUBLANES
    clusters = (mine_ref.shape[0] + theirs_ref.shape[0]) // panel
    shape = (groups, SUBLANES, LANES)
    label = SUBLANES * lax.broadcasted_iota(jnp.int32, shape, 0) + lax.broadcasted_iota(jnp.int32, shape, 1)

    def chunk(i, carry):
        lanes = pl.ds(pl.multiple_of(i * LANES, LANES), LANES)

        def row(value):
            return jnp.broadcast_to(value, (SUBLANES, LANES))

        values, relative = [], []
        for s in range(slots):
            count = jnp.zeros(shape, F32)
            for k in range(negatives):
                count = count + jnp.where(row(neg_ref[s, k : k + 1, lanes])[None] == label, 1.0, 0.0)
            hot = row(pos_ref[s : s + 1, lanes])[None] == label
            live = row(live_ref[s : s + 1, lanes]).astype(F32)[None]
            values.append(jnp.where(hot, -1.0 - count, count) * live)
            relative.append(row(short_ref[s : s + 1, lanes]) ^ me)
        for r in range(clusters):
            block = jnp.zeros(shape, F32)
            for s in range(slots):
                block = jnp.where((relative[s] == r)[None], values[s], block)
            out = theirs_ref if r % 2 else mine_ref
            out[pl.ds((r // 2) * panel, panel), lanes] = block.reshape(panel, LANES).astype(BF16)
        return carry

    lax.fori_loop(0, docs // LANES, chunk, 0)


def score_kernel(*refs, pieces, parts):
    piece_refs = refs[:pieces]
    emb_refs = refs[pieces : pieces + 2]
    target_refs = refs[pieces + 2 : pieces + 4]
    part_refs = refs[pieces + 4 : pieces + 4 + parts]
    dlogit_refs = refs[pieces + 4 + parts : pieces + 6 + parts]
    classifier_ref = refs[pieces + 6 + parts]
    each = piece_refs[0].shape[0]
    for i, ref in enumerate(piece_refs):
        classifier_ref[i * each : (i + 1) * each] = ref[...]
    total = classifier_ref.shape[0]
    rows = min(ROWS, total)
    span = total // parts
    for start in range(0, total, rows):
        block = classifier_ref[start : start + rows]
        grad = None
        for emb_ref, target_ref, dlogit_ref in zip(emb_refs, target_refs, dlogit_refs):
            logits = lax.dot_general(
                block, emb_ref[...], (((1,), (1,)), ((), ())), preferred_element_type=F32
            )
            signed = target_ref[start : start + rows].astype(F32)
            dlogits = (signed * jax.nn.sigmoid(jnp.where(signed < 0, -logits, logits))).astype(BF16)
            dlogit_ref[start : start + rows] = dlogits
            term = jnp.dot(dlogits, emb_ref[...], preferred_element_type=F32)
            grad = term if grad is None else grad + term
        step = min(rows, span)
        for off in range(0, rows, step):
            part, at = divmod(start + off, span)
            ref = part_refs[part]
            ref[at : at + step] = grad[off : off + step].astype(ref.dtype)


def emb_kernel(d_own_ref, d_other_ref, c_own_ref, c_other_ref, out_ref):
    dims = (((0,), (0,)), ((), ()))
    out_ref[...] = lax.dot_general(
        d_own_ref[...], c_own_ref[...], dims, preferred_element_type=F32
    ) + lax.dot_general(d_other_ref[...], c_other_ref[...], dims, preferred_element_type=F32)


def vmem(count):
    return [pl.BlockSpec(memory_space=pltpu.VMEM)] * count


def cost(flops, nbytes):
    return pl.CostEstimate(flops=flops, bytes_accessed=nbytes, transcendentals=0)


def params():
    return pltpu.CompilerParams(vmem_limit_bytes=VMEM_LIMIT)


def shards(embeddings, classifier, label_valid, shortlist, slot_live, positive, negative):
    lab = lax.axis_size("lab")
    enc = lax.axis_size("enc")
    docs, width = embeddings.shape
    panel = classifier.shape[0]
    slots = shortlist.shape[1]
    half = lab // 2 * panel
    groups = bit_groups(lab)

    valid = label_valid.astype(F32)[:, None]
    pieces = [jnp.where(valid > 0, classifier, 0.0).astype(BF16)]
    for group in groups:
        own = pieces[0] if len(pieces) == 1 else jnp.concatenate(pieces, 0)
        pieces = [own] + [flip(own, "lab", mask) for mask in group_masks(group)]

    emb_other = flip(embeddings, "lab", 1)
    target_mine, target_theirs = pl.pallas_call(
        functools.partial(targets_kernel, panel=panel),
        out_shape=[jax.ShapeDtypeStruct((half, docs), BF16)] * 2,
        in_specs=vmem(4),
        out_specs=vmem(2),
        compiler_params=params(),
        cost_estimate=cost(docs * panel * slots * 40, docs * slots * 44 + docs * half * 4),
        name="targets",
    )(shortlist.T, slot_live.T, positive.T, negative.transpose(1, 2, 0))
    target_other = flip(target_theirs, "lab", 1)

    parts = len(group_masks(groups[-1])) + 1 if groups else 1
    outs = pl.pallas_call(
        functools.partial(score_kernel, pieces=len(pieces), parts=parts),
        out_shape=[
            jax.ShapeDtypeStruct((half // parts, width), BF16 if i else F32) for i in range(parts)
        ]
        + [jax.ShapeDtypeStruct((half, docs), BF16)] * 2
        + [jax.ShapeDtypeStruct((half, width), BF16)],
        in_specs=vmem(len(pieces) + 4),
        out_specs=vmem(parts + 3),
        compiler_params=params(),
        cost_estimate=cost(8 * docs * half * width, 4 * docs * width + 8 * half * docs + 8 * half * width),
        name="score",
    )(*pieces, embeddings, emb_other, target_mine, target_other)
    grads, (d_own, d_theirs, classifier_own) = outs[:parts], outs[parts:]

    grad = None
    for group in reversed(groups):
        masks = group_masks(group)
        if grad is not None:
            grad = grad.reshape(len(masks) + 1, -1, width)
            grads = [grad[0]] + [grad[i].astype(BF16) for i in range(1, len(masks) + 1)]
        received = [flip(g, "lab", mask) for g, mask in zip(grads[1:], masks)]
        grad = grads[0]
        for r in received:
            grad = grad + r.astype(F32)
    if grad is None:
        grad = grads[0]
    for bit in range(enc.bit_length() - 1):
        grad = grad + flip(grad.astype(BF16), "enc", 1 << bit).astype(F32)
    w_grad = grad * (valid * (1.0 / math.sqrt(docs * enc * slots)))

    emb_grad = pl.pallas_call(
        emb_kernel,
        out_shape=jax.ShapeDtypeStruct((docs, width), F32),
        in_specs=vmem(4),
        out_specs=pl.BlockSpec(memory_space=pltpu.VMEM),
        compiler_params=params(),
        cost_estimate=cost(4 * docs * half * width, 4 * docs * width + 4 * half * docs + 4 * half * width),
        name="emb_grad",
    )(d_own, flip(d_theirs, "lab", 1), classifier_own, flip(classifier_own, "lab", 1))
    return (w_grad, emb_grad)


def solution(mesh):
    in_specs = (
        P(("enc", "lab"), None),
        P("lab", None),
        P("lab"),
        P(("enc", "lab"), None),
        P(("enc", "lab"), None),
        P(("enc", "lab"), None),
        P(("enc", "lab"), None, None),
    )
    out_specs = (P("lab", None), P(("enc", "lab"), None))
    return jax.shard_map(shards, mesh=mesh, in_specs=in_specs, out_specs=out_specs, check_vma=False)
```

```python
import functools
import math

import jax
import jax.numpy as jnp
from jax import lax
from jax.experimental import pallas as pl
from jax.experimental.pallas import tpu as pltpu
from jax.sharding import PartitionSpec as P

BF16 = jnp.bfloat16
F32 = jnp.float32
LANES = 128
SUBLANES = 8
ROWS = 256
MIB = 1024 * 1024


def flip(value, axis, mask):
    return lax.ppermute(value, axis, [(i, i ^ mask) for i in range(lax.axis_size(axis))])


def bit_groups(count):
    masks = [1 << b for b in range(1, count.bit_length() - 1)]
    return [tuple(masks[i : i + 2]) for i in range(0, len(masks), 2)]


def group_masks(group):
    return [group[0]] if len(group) == 1 else [group[0], group[1], group[0] | group[1]]


def targets_kernel(short_ref, live_ref, pos_ref, neg_ref, mine_ref, theirs_ref, *, panel):
    me = lax.axis_index("lab")
    slots, docs = short_ref.shape
    negatives = neg_ref.shape[1]
    groups = panel // SUBLANES
    clusters = (mine_ref.shape[0] + theirs_ref.shape[0]) // panel
    shape = (groups, SUBLANES, LANES)
    label = SUBLANES * lax.broadcasted_iota(jnp.int32, shape, 0) + lax.broadcasted_iota(jnp.int32, shape, 1)

    def chunk(i, carry):
        lanes = pl.ds(pl.multiple_of(i * LANES, LANES), LANES)

        def row(value):
            return jnp.broadcast_to(value, (SUBLANES, LANES))

        values, relative = [], []
        for s in range(slots):
            count = jnp.zeros(shape, F32)
            for k in range(negatives):
                count = count + jnp.where(row(neg_ref[s, k : k + 1, lanes])[None] == label, 1.0, 0.0)
            hot = row(pos_ref[s : s + 1, lanes])[None] == label
            live = row(live_ref[s : s + 1, lanes]).astype(F32)[None]
            values.append(jnp.where(hot, -1.0 - count, count) * live)
            relative.append(row(short_ref[s : s + 1, lanes]) ^ me)
        for r in range(clusters):
            block = jnp.zeros(shape, F32)
            for s in range(slots):
                block = jnp.where((relative[s] == r)[None], values[s], block)
            out = theirs_ref if r % 2 else mine_ref
            out[pl.ds((r // 2) * panel, panel), lanes] = block.reshape(panel, LANES).astype(BF16)
        return carry

    lax.fori_loop(0, docs // LANES, chunk, 0)


def pack_kernel(classifier_ref, valid_ref, out_ref):
    panel = classifier_ref.shape[0]
    diagonal = lax.broadcasted_iota(jnp.int32, (panel, panel), 0) == lax.broadcasted_iota(
        jnp.int32, (panel, panel), 1
    )
    flags = jnp.broadcast_to(valid_ref[...].astype(F32), (panel, panel))
    column = jnp.sum(jnp.where(diagonal, flags, 0.0), axis=1, keepdims=True)
    out_ref[...] = (classifier_ref[...] * column).astype(BF16)


def score_kernel(*refs, pieces, parts):
    piece_refs = refs[:pieces]
    emb_refs = refs[pieces : pieces + 2]
    target_refs = refs[pieces + 2 : pieces + 4]
    part_refs = refs[pieces + 4 : pieces + 4 + parts]
    dlogit_refs = refs[pieces + 4 + parts : pieces + 6 + parts]
    classifier_ref = refs[pieces + 6 + parts]
    each = piece_refs[0].shape[0]
    for i, ref in enumerate(piece_refs):
        classifier_ref[i * each : (i + 1) * each] = ref[...]
    total = classifier_ref.shape[0]
    rows = min(ROWS, total)
    span = total // parts
    for start in range(0, total, rows):
        block = classifier_ref[start : start + rows]
        grad = None
        for emb_ref, target_ref, dlogit_ref in zip(emb_refs, target_refs, dlogit_refs):
            logits = lax.dot_general(
                block, emb_ref[...], (((1,), (1,)), ((), ())), preferred_element_type=F32
            )
            signed = target_ref[start : start + rows].astype(F32)
            dlogits = (signed * jax.nn.sigmoid(jnp.where(signed < 0, -logits, logits))).astype(BF16)
            dlogit_ref[start : start + rows] = dlogits
            term = jnp.dot(dlogits, emb_ref[...], preferred_element_type=F32)
            grad = term if grad is None else grad + term
        step = min(rows, span)
        for off in range(0, rows, step):
            part, at = divmod(start + off, span)
            ref = part_refs[part]
            ref[at : at + step] = grad[off : off + step].astype(ref.dtype)


def emb_kernel(d_own_ref, d_other_ref, c_own_ref, c_other_ref, out_ref):
    dims = (((0,), (0,)), ((), ()))
    out_ref[...] = lax.dot_general(
        d_own_ref[...], c_own_ref[...], dims, preferred_element_type=F32
    ) + lax.dot_general(d_other_ref[...], c_other_ref[...], dims, preferred_element_type=F32)


def vmem(count):
    return [pl.BlockSpec(memory_space=pltpu.VMEM)] * count


def cost(flops, nbytes):
    return pl.CostEstimate(flops=flops, bytes_accessed=nbytes, transcendentals=0)


def params(*sizes):
    return pltpu.CompilerParams(vmem_limit_bytes=(2 * sum(sizes) // MIB + 4) * MIB)


def shards(embeddings, classifier, label_valid, shortlist, slot_live, positive, negative):
    lab = lax.axis_size("lab")
    enc = lax.axis_size("enc")
    docs, width = embeddings.shape
    panel = classifier.shape[0]
    slots = shortlist.shape[1]
    half = lab // 2 * panel
    groups = bit_groups(lab)

    pieces = [
        pl.pallas_call(
            pack_kernel,
            out_shape=jax.ShapeDtypeStruct((panel, width), BF16),
            in_specs=vmem(2),
            out_specs=pl.BlockSpec(memory_space=pltpu.VMEM),
            compiler_params=params(panel * width * 6),
            cost_estimate=cost(panel * width, panel * width * 6),
            name="pack",
        )(classifier, label_valid.reshape(1, panel))
    ]
    for group in groups:
        own = pieces[0] if len(pieces) == 1 else jnp.concatenate(pieces, 0)
        pieces = [own] + [flip(own, "lab", mask) for mask in group_masks(group)]

    emb_other = flip(embeddings, "lab", 1)
    target_mine, target_theirs = pl.pallas_call(
        functools.partial(targets_kernel, panel=panel),
        out_shape=[jax.ShapeDtypeStruct((half, docs), BF16)] * 2,
        in_specs=vmem(4),
        out_specs=vmem(2),
        compiler_params=params(docs * slots * 44, docs * half * 4),
        cost_estimate=cost(docs * panel * slots * 40, docs * slots * 44 + docs * half * 4),
        name="targets",
    )(shortlist.T, slot_live.T, positive.T, negative.transpose(1, 2, 0))
    target_other = flip(target_theirs, "lab", 1)

    parts = len(group_masks(groups[-1])) + 1 if groups else 1
    outs = pl.pallas_call(
        functools.partial(score_kernel, pieces=len(pieces), parts=parts),
        out_shape=[
            jax.ShapeDtypeStruct((half // parts, width), BF16 if i else F32) for i in range(parts)
        ]
        + [jax.ShapeDtypeStruct((half, docs), BF16)] * 2
        + [jax.ShapeDtypeStruct((half, width), BF16)],
        in_specs=vmem(len(pieces) + 4),
        out_specs=vmem(parts + 3),
        compiler_params=params(4 * docs * width, 16 * half * docs, 12 * half * width),
        cost_estimate=cost(8 * docs * half * width, 4 * docs * width + 8 * half * docs + 8 * half * width),
        name="score",
    )(*pieces, embeddings, emb_other, target_mine, target_other)
    grads, (d_own, d_theirs, classifier_own) = outs[:parts], outs[parts:]

    grad = None
    for group in reversed(groups):
        masks = group_masks(group)
        if grad is not None:
            grad = grad.reshape(len(masks) + 1, -1, width)
            grads = [grad[0]] + [grad[i].astype(BF16) for i in range(1, len(masks) + 1)]
        received = [flip(g, "lab", mask) for g, mask in zip(grads[1:], masks)]
        grad = grads[0]
        for r in received:
            grad = grad + r.astype(F32)
    if grad is None:
        grad = grads[0]
    for bit in range(enc.bit_length() - 1):
        grad = grad + flip(grad.astype(BF16), "enc", 1 << bit).astype(F32)
    w_grad = grad * (label_valid.astype(F32) * (1.0 / math.sqrt(docs * enc * slots)))[:, None]

    emb_grad = pl.pallas_call(
        emb_kernel,
        out_shape=jax.ShapeDtypeStruct((docs, width), F32),
        in_specs=vmem(4),
        out_specs=pl.BlockSpec(memory_space=pltpu.VMEM),
        compiler_params=params(8 * docs * width, 4 * half * docs, 4 * half * width),
        cost_estimate=cost(4 * docs * half * width, 4 * docs * width + 4 * half * docs + 4 * half * width),
        name="emb_grad",
    )(d_own, flip(d_theirs, "lab", 1), classifier_own, flip(classifier_own, "lab", 1))
    return (w_grad, emb_grad)


def solution(mesh):
    in_specs = (
        P(("enc", "lab"), None),
        P("lab", None),
        P("lab"),
        P(("enc", "lab"), None),
        P(("enc", "lab"), None),
        P(("enc", "lab"), None),
        P(("enc", "lab"), None, None),
    )
    out_specs = (P("lab", None), P(("enc", "lab"), None))
    return jax.shard_map(shards, mesh=mesh, in_specs=in_specs, out_specs=out_specs, check_vma=False)
```

```python
import functools
import math

import jax
import jax.numpy as jnp
from jax import lax
from jax.experimental import pallas as pl
from jax.experimental.pallas import tpu as pltpu
from jax.sharding import PartitionSpec as P

BF16 = jnp.bfloat16
F32 = jnp.float32
LANES = 128
SUBLANES = 8
ROWS = 256
MIB = 1024 * 1024


def flip(value, axis, mask):
    return lax.ppermute(value, axis, [(i, i ^ mask) for i in range(lax.axis_size(axis))])


def bit_groups(count):
    masks = [1 << b for b in range(1, count.bit_length() - 1)]
    return [tuple(masks[i : i + 2]) for i in range(0, len(masks), 2)]


def group_masks(group):
    return [group[0]] if len(group) == 1 else [group[0], group[1], group[0] | group[1]]


def fetch(sources, targets, sem):
    copies = [pltpu.make_async_copy(x, y, sem.at[i]) for i, (x, y) in enumerate(zip(sources, targets))]
    for copy in copies:
        copy.start()
    for copy in copies:
        copy.wait()


def flag_column(flags):
    panel = flags.shape[1]
    diagonal = lax.broadcasted_iota(jnp.int32, (panel, panel), 0) == lax.broadcasted_iota(
        jnp.int32, (panel, panel), 1
    )
    spread = jnp.broadcast_to(flags.astype(F32), (panel, panel))
    return jnp.sum(jnp.where(diagonal, spread, 0.0), axis=1, keepdims=True)


def pack_kernel(classifier_hbm, valid_hbm, out_ref, classifier_ref, valid_ref, sem):
    fetch((classifier_hbm, valid_hbm), (classifier_ref, valid_ref), sem)
    out_ref[...] = (classifier_ref[...] * flag_column(valid_ref[...])).astype(BF16)


def targets_kernel(
    short_hbm, live_hbm, pos_hbm, neg_hbm, emb_hbm, after_ref, mine_ref, theirs_ref, emb_ref,
    short_ref, live_ref, pos_ref, neg_ref, sem, emb_sem, *, panel
):
    emb_copy = pltpu.make_async_copy(emb_hbm, emb_ref, emb_sem)
    emb_copy.start()
    fetch((short_hbm, live_hbm, pos_hbm, neg_hbm), (short_ref, live_ref, pos_ref, neg_ref), sem)
    me = lax.axis_index("lab")
    slots, docs = short_ref.shape
    negatives = neg_ref.shape[1]
    groups = panel // SUBLANES
    clusters = (mine_ref.shape[0] + theirs_ref.shape[0]) // panel
    shape = (groups, SUBLANES, LANES)
    label = SUBLANES * lax.broadcasted_iota(jnp.int32, shape, 0) + lax.broadcasted_iota(jnp.int32, shape, 1)

    def chunk(i, carry):
        lanes = pl.ds(pl.multiple_of(i * LANES, LANES), LANES)

        def row(value):
            return jnp.broadcast_to(value, (SUBLANES, LANES))

        values, relative = [], []
        for s in range(slots):
            count = jnp.zeros(shape, F32)
            for k in range(negatives):
                count = count + jnp.where(row(neg_ref[s, k : k + 1, lanes])[None] == label, 1.0, 0.0)
            hot = row(pos_ref[s : s + 1, lanes])[None] == label
            live = row(live_ref[s : s + 1, lanes]).astype(F32)[None]
            values.append(jnp.where(hot, -1.0 - count, count) * live)
            relative.append(row(short_ref[s : s + 1, lanes]) ^ me)
        for r in range(clusters):
            block = jnp.zeros(shape, F32)
            for s in range(slots):
                block = jnp.where((relative[s] == r)[None], values[s], block)
            out = theirs_ref if r % 2 else mine_ref
            out[pl.ds((r // 2) * panel, panel), lanes] = block.reshape(panel, LANES).astype(BF16)
        return carry

    lax.fori_loop(0, docs // LANES, chunk, 0)
    emb_copy.wait()


def score_kernel(*refs, pieces, parts):
    piece_refs = refs[:pieces]
    emb_refs = refs[pieces : pieces + 2]
    target_refs = refs[pieces + 2 : pieces + 4]
    part_refs = refs[pieces + 4 : pieces + 4 + parts]
    dlogit_refs = refs[pieces + 4 + parts : pieces + 6 + parts]
    classifier_ref = refs[pieces + 6 + parts]
    each = piece_refs[0].shape[0]
    for i, ref in enumerate(piece_refs):
        classifier_ref[i * each : (i + 1) * each] = ref[...]
    total = classifier_ref.shape[0]
    rows = min(ROWS, total)
    span = total // parts
    for start in range(0, total, rows):
        block = classifier_ref[start : start + rows]
        grad = None
        for emb_ref, target_ref, dlogit_ref in zip(emb_refs, target_refs, dlogit_refs):
            logits = lax.dot_general(
                block, emb_ref[...], (((1,), (1,)), ((), ())), preferred_element_type=F32
            )
            signed = target_ref[start : start + rows].astype(F32)
            dlogits = (signed * jax.nn.sigmoid(jnp.where(signed < 0, -logits, logits))).astype(BF16)
            dlogit_ref[start : start + rows] = dlogits
            term = jnp.dot(dlogits, emb_ref[...], preferred_element_type=F32)
            grad = term if grad is None else grad + term
        step = min(rows, span)
        for off in range(0, rows, step):
            part, at = divmod(start + off, span)
            ref = part_refs[part]
            ref[at : at + step] = grad[off : off + step].astype(ref.dtype)


def emb_kernel(d_own_ref, d_other_ref, c_own_ref, c_other_ref, after_ref, out_ref):
    dims = (((0,), (0,)), ((), ()))
    out_ref[...] = lax.dot_general(
        d_own_ref[...], c_own_ref[...], dims, preferred_element_type=F32
    ) + lax.dot_general(d_other_ref[...], c_other_ref[...], dims, preferred_element_type=F32)


def finish_kernel(grad_ref, received_ref, valid_hbm, after_hbm, out_ref, valid_ref, sem, *, scale):
    fetch((valid_hbm,), (valid_ref,), sem)
    column = flag_column(valid_ref[...]) * scale
    out_ref[...] = (grad_ref[...] + received_ref[...].astype(F32)) * column


def hbm(count):
    return [pl.BlockSpec(memory_space=pltpu.HBM)] * count


def vmem(count):
    return [pl.BlockSpec(memory_space=pltpu.VMEM)] * count


def keep(*arrays):
    return [pltpu.with_memory_space_constraint(x, pltpu.HBM) for x in arrays]


def cost(flops, nbytes):
    return pl.CostEstimate(flops=flops, bytes_accessed=nbytes, transcendentals=0)


def params(*sizes):
    return pltpu.CompilerParams(vmem_limit_bytes=(2 * sum(sizes) // MIB + 4) * MIB)


def shards(embeddings, classifier, label_valid, shortlist, slot_live, positive, negative):
    lab = lax.axis_size("lab")
    enc = lax.axis_size("enc")
    docs, width = embeddings.shape
    panel = classifier.shape[0]
    slots = shortlist.shape[1]
    half = lab // 2 * panel
    groups = bit_groups(lab)

    valid = label_valid.reshape(1, panel)
    packed = pl.pallas_call(
        pack_kernel,
        out_shape=jax.ShapeDtypeStruct((panel, width), BF16),
        in_specs=hbm(2),
        out_specs=pl.BlockSpec(memory_space=pltpu.VMEM),
        scratch_shapes=[
            pltpu.VMEM((panel, width), F32),
            pltpu.VMEM((1, panel), jnp.int32),
            pltpu.SemaphoreType.DMA((2,)),
        ],
        compiler_params=params(panel * width * 6),
        cost_estimate=cost(panel * width, panel * width * 6),
        name="pack",
    )(*keep(classifier, valid))
    pieces = [packed]
    for group in groups:
        own = pieces[0] if len(pieces) == 1 else jnp.concatenate(pieces, 0)
        pieces = [own] + [flip(own, "lab", mask) for mask in group_masks(group)]

    emb_other = flip(embeddings, "lab", 1)
    target_mine, target_theirs, emb_own = pl.pallas_call(
        functools.partial(targets_kernel, panel=panel),
        out_shape=[jax.ShapeDtypeStruct((half, docs), BF16)] * 2
        + [jax.ShapeDtypeStruct((docs, width), BF16)],
        in_specs=hbm(5) + vmem(1),
        out_specs=vmem(3),
        scratch_shapes=[pltpu.VMEM((slots, docs), jnp.int32)] * 3
        + [
            pltpu.VMEM((slots, negative.shape[2], docs), jnp.int32),
            pltpu.SemaphoreType.DMA((4,)),
            pltpu.SemaphoreType.DMA,
        ],
        compiler_params=params(docs * slots * 44, docs * half * 4, docs * width * 2),
        cost_estimate=cost(docs * panel * slots * 40, docs * slots * 44 + docs * half * 4),
        name="targets",
    )(*keep(shortlist.T, slot_live.T, positive.T, negative.transpose(1, 2, 0), embeddings), packed)
    target_other = flip(target_theirs, "lab", 1)

    parts = len(group_masks(groups[-1])) + 1 if groups else 1
    outs = pl.pallas_call(
        functools.partial(score_kernel, pieces=len(pieces), parts=parts),
        out_shape=[
            jax.ShapeDtypeStruct((half // parts, width), BF16 if i else F32) for i in range(parts)
        ]
        + [jax.ShapeDtypeStruct((half, docs), BF16)] * 2
        + [jax.ShapeDtypeStruct((half, width), BF16)],
        in_specs=vmem(len(pieces) + 4),
        out_specs=vmem(parts + 3),
        compiler_params=params(4 * docs * width, 16 * half * docs, 12 * half * width),
        cost_estimate=cost(8 * docs * half * width, 4 * docs * width + 8 * half * docs + 8 * half * width),
        name="score",
    )(*pieces, emb_own, emb_other, target_mine, target_other)
    grads, (d_own, d_theirs, classifier_own) = outs[:parts], outs[parts:]

    grad = None
    for group in reversed(groups):
        masks = group_masks(group)
        if grad is not None:
            grad = grad.reshape(len(masks) + 1, -1, width)
            grads = [grad[0]] + [grad[i].astype(BF16) for i in range(1, len(masks) + 1)]
        received = [flip(g, "lab", mask) for g, mask in zip(grads[1:], masks)]
        grad = grads[0]
        for r in received:
            grad = grad + r.astype(F32)
    if grad is None:
        grad = grads[0]
    d_other, classifier_other = flip(d_theirs, "lab", 1), flip(classifier_own, "lab", 1)
    bits = [1 << bit for bit in range(enc.bit_length() - 1)]
    for bit in bits[:-1]:
        grad = grad + flip(grad.astype(BF16), "enc", bit).astype(F32)
    received = flip(grad.astype(BF16), "enc", bits[-1])

    emb_grad = pl.pallas_call(
        emb_kernel,
        out_shape=jax.ShapeDtypeStruct((docs, width), F32),
        in_specs=vmem(5),
        out_specs=pl.BlockSpec(memory_space=pltpu.VMEM),
        compiler_params=params(8 * docs * width, 4 * half * docs, 4 * half * width),
        cost_estimate=cost(4 * docs * half * width, 4 * docs * width + 4 * half * docs + 4 * half * width),
        name="emb_grad",
    )(d_own, d_other, classifier_own, classifier_other, grad)

    w_grad = pl.pallas_call(
        functools.partial(finish_kernel, scale=1.0 / math.sqrt(docs * enc * slots)),
        out_shape=jax.ShapeDtypeStruct((panel, width), F32),
        in_specs=vmem(2) + hbm(2),
        out_specs=pl.BlockSpec(memory_space=pltpu.VMEM),
        scratch_shapes=[pltpu.VMEM((1, panel), jnp.int32), pltpu.SemaphoreType.DMA((1,))],
        compiler_params=params(panel * width * 10),
        cost_estimate=cost(panel * width, panel * width * 10),
        name="finish",
    )(grad, received, *keep(valid, emb_grad))
    return (w_grad, emb_grad)


def solution(mesh):
    in_specs = (
        P(("enc", "lab"), None),
        P("lab", None),
        P("lab"),
        P(("enc", "lab"), None),
        P(("enc", "lab"), None),
        P(("enc", "lab"), None),
        P(("enc", "lab"), None, None),
    )
    out_specs = (P("lab", None), P(("enc", "lab"), None))
    return jax.shard_map(shards, mesh=mesh, in_specs=in_specs, out_specs=out_specs, check_vma=False)
```

```python
import functools
import math

import jax
import jax.numpy as jnp
from jax import lax
from jax.experimental import pallas as pl
from jax.experimental.pallas import tpu as pltpu
from jax.sharding import PartitionSpec as P

BF16 = jnp.bfloat16
F32 = jnp.float32
LANES = 128
SUBLANES = 8
ROWS = 256
MIB = 1024 * 1024


def flip(value, axis, mask):
    return lax.ppermute(value, axis, [(i, i ^ mask) for i in range(lax.axis_size(axis))])


def bit_groups(count):
    masks = [1 << b for b in range(1, count.bit_length() - 1)]
    return [tuple(masks[i : i + 2]) for i in range(0, len(masks), 2)]


def group_masks(group):
    return [group[0]] if len(group) == 1 else [group[0], group[1], group[0] | group[1]]


def fetch(sources, targets, sem):
    copies = [pltpu.make_async_copy(x, y, sem.at[i]) for i, (x, y) in enumerate(zip(sources, targets))]
    for copy in copies:
        copy.start()
    for copy in copies:
        copy.wait()


def flag_column(flags):
    panel = flags.shape[1]
    diagonal = lax.broadcasted_iota(jnp.int32, (panel, panel), 0) == lax.broadcasted_iota(
        jnp.int32, (panel, panel), 1
    )
    spread = jnp.broadcast_to(flags.astype(F32), (panel, panel))
    return jnp.sum(jnp.where(diagonal, spread, 0.0), axis=1, keepdims=True)


def pack_kernel(
    classifier_hbm, valid_hbm, short_hbm, live_hbm, pos_hbm, neg_hbm, rows_ref, column_ref, index_ref,
    classifier_ref, valid_ref, short_ref, live_ref, pos_ref, sem, *, scale
):
    slots, negatives, docs = neg_hbm.shape
    fetch(
        (classifier_hbm, valid_hbm, short_hbm, live_hbm, pos_hbm)
        + tuple(neg_hbm.at[s] for s in range(slots)),
        (classifier_ref, valid_ref, short_ref, live_ref, pos_ref)
        + tuple(index_ref.at[pl.ds(s * negatives, negatives)] for s in range(slots)),
        sem,
    )
    column = flag_column(valid_ref[...])
    rows_ref[...] = (classifier_ref[...] * column).astype(BF16)
    column_ref[...] = jnp.broadcast_to(column * scale, column_ref.shape)
    index_ref[slots * negatives : slots * (negatives + 2)] = jnp.concatenate(
        [pos_ref[...], jnp.where(live_ref[...] > 0, short_ref[...], -1)], 0
    )


def targets_kernel(
    index_own_ref, index_other_ref, emb_hbm, target_own_ref, target_other_ref, emb_ref, emb_sem, *, panel, slots
):
    emb_copy = pltpu.make_async_copy(emb_hbm, emb_ref, emb_sem)
    emb_copy.start()
    me = lax.axis_index("lab")
    docs = index_own_ref.shape[1]
    negatives = index_own_ref.shape[0] // slots - 2
    groups = panel // SUBLANES
    shape = (groups, SUBLANES, LANES)
    label = SUBLANES * lax.broadcasted_iota(jnp.int32, shape, 0) + lax.broadcasted_iota(jnp.int32, shape, 1)

    def fill(index_ref, out_ref, lanes):
        def row(at):
            return jnp.broadcast_to(index_ref[at : at + 1, lanes], (SUBLANES, LANES))

        values, relative = [], []
        for s in range(slots):
            count = jnp.zeros(shape, F32)
            for k in range(negatives):
                count = count + jnp.where(row(s * negatives + k)[None] == label, 1.0, 0.0)
            hot = row(slots * negatives + s)[None] == label
            values.append(jnp.where(hot, -1.0 - count, count))
            relative.append(row(slots * (negatives + 1) + s) ^ me)
        for j in range(out_ref.shape[0] // panel):
            block = jnp.zeros(shape, F32)
            for s in range(slots):
                block = jnp.where((relative[s] == 2 * j)[None], values[s], block)
            out_ref[pl.ds(j * panel, panel), lanes] = block.reshape(panel, LANES).astype(BF16)

    def chunk(i, carry):
        lanes = pl.ds(pl.multiple_of(i * LANES, LANES), LANES)
        fill(index_own_ref, target_own_ref, lanes)
        fill(index_other_ref, target_other_ref, lanes)
        return carry

    lax.fori_loop(0, docs // LANES, chunk, 0)
    emb_copy.wait()


def score_kernel(*refs, pieces, parts):
    piece_refs = refs[:pieces]
    emb_refs = refs[pieces : pieces + 2]
    target_refs = refs[pieces + 2 : pieces + 4]
    part_refs = refs[pieces + 4 : pieces + 4 + parts]
    dlogit_refs = refs[pieces + 4 + parts : pieces + 6 + parts]
    classifier_ref = refs[pieces + 6 + parts]
    each = piece_refs[0].shape[0]
    for i, ref in enumerate(piece_refs):
        classifier_ref[i * each : (i + 1) * each] = ref[...]
    total = classifier_ref.shape[0]
    rows = min(ROWS, total)
    span = total // parts
    for start in range(0, total, rows):
        block = classifier_ref[start : start + rows]
        grad = None
        for emb_ref, target_ref, dlogit_ref in zip(emb_refs, target_refs, dlogit_refs):
            logits = lax.dot_general(
                block, emb_ref[...], (((1,), (1,)), ((), ())), preferred_element_type=F32
            )
            signed = target_ref[start : start + rows].astype(F32)
            dlogits = (signed * jax.nn.sigmoid(jnp.where(signed < 0, -logits, logits))).astype(BF16)
            dlogit_ref[start : start + rows] = dlogits
            term = jnp.dot(dlogits, emb_ref[...], preferred_element_type=F32)
            grad = term if grad is None else grad + term
        step = min(rows, span)
        for off in range(0, rows, step):
            part, at = divmod(start + off, span)
            ref = part_refs[part]
            ref[at : at + step] = grad[off : off + step].astype(ref.dtype)


def emb_kernel(d_own_ref, d_other_ref, c_own_ref, c_other_ref, after_ref, out_ref):
    dims = (((0,), (0,)), ((), ()))
    out_ref[...] = lax.dot_general(
        d_own_ref[...], c_own_ref[...], dims, preferred_element_type=F32
    ) + lax.dot_general(d_other_ref[...], c_other_ref[...], dims, preferred_element_type=F32)


def finish_kernel(grad_ref, received_ref, column_ref, after_hbm, out_ref):
    out_ref[...] = (grad_ref[...] + received_ref[...].astype(F32)) * column_ref[:, :1]


def hbm(count):
    return [pl.BlockSpec(memory_space=pltpu.HBM)] * count


def vmem(count):
    return [pl.BlockSpec(memory_space=pltpu.VMEM)] * count


def keep(*arrays):
    return [pltpu.with_memory_space_constraint(x, pltpu.HBM) for x in arrays]


def cost(flops, nbytes):
    return pl.CostEstimate(flops=flops, bytes_accessed=nbytes, transcendentals=0)


def params(*sizes):
    return pltpu.CompilerParams(vmem_limit_bytes=(2 * sum(sizes) // MIB + 4) * MIB)


def shards(embeddings, classifier, label_valid, shortlist, slot_live, positive, negative):
    lab = lax.axis_size("lab")
    enc = lax.axis_size("enc")
    docs, width = embeddings.shape
    panel = classifier.shape[0]
    slots = shortlist.shape[1]
    half = lab // 2 * panel
    groups = bit_groups(lab)

    negatives = negative.shape[2]
    height = slots * (negatives + 2)
    packed, column, index_own = pl.pallas_call(
        functools.partial(pack_kernel, scale=1.0 / math.sqrt(docs * enc * slots)),
        out_shape=[
            jax.ShapeDtypeStruct((panel, width), BF16),
            jax.ShapeDtypeStruct((panel, LANES), F32),
            jax.ShapeDtypeStruct((height, docs), jnp.int32),
        ],
        in_specs=hbm(6),
        out_specs=vmem(3),
        scratch_shapes=[pltpu.VMEM((panel, width), F32), pltpu.VMEM((1, panel), jnp.int32)]
        + [pltpu.VMEM((slots, docs), jnp.int32)] * 3
        + [pltpu.SemaphoreType.DMA((5 + slots,))],
        compiler_params=params(panel * width * 6, height * docs * 4),
        cost_estimate=cost(panel * width, panel * width * 6 + height * docs * 4),
        name="pack",
    )(
        *keep(
            classifier, label_valid.reshape(1, panel), shortlist.T, slot_live.T, positive.T,
            negative.transpose(1, 2, 0),
        )
    )
    pieces = [packed]
    for group in groups:
        own = pieces[0] if len(pieces) == 1 else jnp.concatenate(pieces, 0)
        pieces = [own] + [flip(own, "lab", mask) for mask in group_masks(group)]

    emb_other = flip(embeddings, "lab", 1)
    index_other = flip(index_own, "lab", 1)
    target_own, target_other, emb_own = pl.pallas_call(
        functools.partial(targets_kernel, panel=panel, slots=slots),
        out_shape=[jax.ShapeDtypeStruct((half, docs), BF16)] * 2
        + [jax.ShapeDtypeStruct((docs, width), BF16)],
        in_specs=vmem(2) + hbm(1),
        out_specs=vmem(3),
        scratch_shapes=[pltpu.SemaphoreType.DMA],
        compiler_params=params(height * docs * 8, docs * half * 4, docs * width * 2),
        cost_estimate=cost(docs * panel * slots * 80, height * docs * 8 + docs * half * 4),
        name="targets",
    )(index_own, index_other, *keep(embeddings))
    parts = len(group_masks(groups[-1])) + 1 if groups else 1
    outs = pl.pallas_call(
        functools.partial(score_kernel, pieces=len(pieces), parts=parts),
        out_shape=[
            jax.ShapeDtypeStruct((half // parts, width), BF16 if i else F32) for i in range(parts)
        ]
        + [jax.ShapeDtypeStruct((half, docs), BF16)] * 2
        + [jax.ShapeDtypeStruct((half, width), BF16)],
        in_specs=vmem(len(pieces) + 4),
        out_specs=vmem(parts + 3),
        compiler_params=params(4 * docs * width, 16 * half * docs, 12 * half * width),
        cost_estimate=cost(8 * docs * half * width, 4 * docs * width + 8 * half * docs + 8 * half * width),
        name="score",
    )(*pieces, emb_own, emb_other, target_own, target_other)
    grads, (d_own, d_theirs, classifier_own) = outs[:parts], outs[parts:]

    grad = None
    for group in reversed(groups):
        masks = group_masks(group)
        if grad is not None:
            grad = grad.reshape(len(masks) + 1, -1, width)
            grads = [grad[0]] + [grad[i].astype(BF16) for i in range(1, len(masks) + 1)]
        received = [flip(g, "lab", mask) for g, mask in zip(grads[1:], masks)]
        grad = grads[0]
        for r in received:
            grad = grad + r.astype(F32)
    if grad is None:
        grad = grads[0]
    d_other, classifier_other = flip(d_theirs, "lab", 1), flip(classifier_own, "lab", 1)
    bits = [1 << bit for bit in range(enc.bit_length() - 1)]
    for bit in bits[:-1]:
        grad = grad + flip(grad.astype(BF16), "enc", bit).astype(F32)
    received = flip(grad.astype(BF16), "enc", bits[-1])

    emb_grad = pl.pallas_call(
        emb_kernel,
        out_shape=jax.ShapeDtypeStruct((docs, width), F32),
        in_specs=vmem(5),
        out_specs=pl.BlockSpec(memory_space=pltpu.VMEM),
        compiler_params=params(8 * docs * width, 4 * half * docs, 4 * half * width),
        cost_estimate=cost(4 * docs * half * width, 4 * docs * width + 4 * half * docs + 4 * half * width),
        name="emb_grad",
    )(d_own, d_other, classifier_own, classifier_other, grad)

    w_grad = pl.pallas_call(
        finish_kernel,
        out_shape=jax.ShapeDtypeStruct((panel, width), F32),
        in_specs=vmem(3) + hbm(1),
        out_specs=pl.BlockSpec(memory_space=pltpu.VMEM),
        compiler_params=params(panel * width * 10),
        cost_estimate=cost(panel * width, panel * width * 10),
        name="finish",
    )(grad, received, column, *keep(emb_grad))
    return (w_grad, emb_grad)


def solution(mesh):
    in_specs = (
        P(("enc", "lab"), None),
        P("lab", None),
        P("lab"),
        P(("enc", "lab"), None),
        P(("enc", "lab"), None),
        P(("enc", "lab"), None),
        P(("enc", "lab"), None, None),
    )
    out_specs = (P("lab", None), P(("enc", "lab"), None))
    return jax.shard_map(shards, mesh=mesh, in_specs=in_specs, out_specs=out_specs, check_vma=False)
```

```python
import functools
import math

import jax
import jax.numpy as jnp
from jax import lax
from jax.experimental import pallas as pl
from jax.experimental.pallas import tpu as pltpu
from jax.sharding import PartitionSpec as P

BF16 = jnp.bfloat16
F32 = jnp.float32
LANES = 128
SUBLANES = 8
ROWS = 256
MIB = 1024 * 1024


def flip(value, axis, mask):
    return lax.ppermute(value, axis, [(i, i ^ mask) for i in range(lax.axis_size(axis))])


def bit_groups(count):
    masks = [1 << b for b in range(1, count.bit_length() - 1)]
    return [tuple(masks[i : i + 2]) for i in range(0, len(masks), 2)]


def group_masks(group):
    return [group[0]] if len(group) == 1 else [group[0], group[1], group[0] | group[1]]


def fetch(sources, targets, sem):
    copies = [pltpu.make_async_copy(x, y, sem.at[i]) for i, (x, y) in enumerate(zip(sources, targets))]
    for copy in copies:
        copy.start()
    for copy in copies:
        copy.wait()


def flag_column(flags):
    panel = flags.shape[1]
    diagonal = lax.broadcasted_iota(jnp.int32, (panel, panel), 0) == lax.broadcasted_iota(
        jnp.int32, (panel, panel), 1
    )
    spread = jnp.broadcast_to(flags.astype(F32), (panel, panel))
    return jnp.sum(jnp.where(diagonal, spread, 0.0), axis=1, keepdims=True)


def pack_kernel(
    classifier_hbm, valid_hbm, short_hbm, live_hbm, pos_hbm, neg_hbm, rows_ref, column_ref, index_ref,
    classifier_ref, valid_ref, short_ref, live_ref, pos_ref, sem, *, scale
):
    slots, negatives, docs = neg_hbm.shape
    fetch(
        (classifier_hbm, valid_hbm, short_hbm, live_hbm, pos_hbm)
        + tuple(neg_hbm.at[s] for s in range(slots)),
        (classifier_ref, valid_ref, short_ref, live_ref, pos_ref)
        + tuple(index_ref.at[pl.ds(s * negatives, negatives)] for s in range(slots)),
        sem,
    )
    column = flag_column(valid_ref[...])
    rows_ref[...] = (classifier_ref[...] * column).astype(BF16)
    column_ref[...] = jnp.broadcast_to(column * scale, column_ref.shape)
    index_ref[slots * negatives : slots * (negatives + 2)] = jnp.concatenate(
        [pos_ref[...], jnp.where(live_ref[...] > 0, short_ref[...], -1)], 0
    )


def turn_kernel(emb_hbm, other_ref, own_ref, own_turned_ref, other_turned_ref, sem):
    copy = pltpu.make_async_copy(emb_hbm, own_ref, sem)
    copy.start()
    other_turned_ref[...] = other_ref[...].T
    copy.wait()
    own_turned_ref[...] = own_ref[...].T


def targets_kernel(index_own_ref, index_other_ref, after_ref, target_own_ref, target_other_ref, *, panel, slots):
    me = lax.axis_index("lab")
    docs = index_own_ref.shape[1]
    negatives = index_own_ref.shape[0] // slots - 2
    groups = panel // SUBLANES
    shape = (groups, SUBLANES, LANES)
    label = SUBLANES * lax.broadcasted_iota(jnp.int32, shape, 0) + lax.broadcasted_iota(jnp.int32, shape, 1)

    def fill(index_ref, out_ref, lanes):
        def row(at):
            return jnp.broadcast_to(index_ref[at : at + 1, lanes], (SUBLANES, LANES))

        values, relative = [], []
        for s in range(slots):
            count = jnp.zeros(shape, F32)
            for k in range(negatives):
                count = count + jnp.where(row(s * negatives + k)[None] == label, 1.0, 0.0)
            hot = row(slots * negatives + s)[None] == label
            values.append(jnp.where(hot, -1.0 - count, count))
            relative.append(row(slots * (negatives + 1) + s) ^ me)
        for j in range(out_ref.shape[0] // panel):
            block = jnp.zeros(shape, F32)
            for s in range(slots):
                block = jnp.where((relative[s] == 2 * j)[None], values[s], block)
            out_ref[pl.ds(j * panel, panel), lanes] = block.reshape(panel, LANES).astype(BF16)

    def chunk(i, carry):
        lanes = pl.ds(pl.multiple_of(i * LANES, LANES), LANES)
        fill(index_own_ref, target_own_ref, lanes)
        fill(index_other_ref, target_other_ref, lanes)
        return carry

    lax.fori_loop(0, docs // LANES, chunk, 0)


def score_kernel(*refs, which, after):
    refs = list(refs)

    def take(number):
        return [refs.pop(0) for _ in range(number)]

    count = len(which)
    piece_refs, emb_refs, turned_refs, target_refs = take(count), take(2), take(2), take(2)
    take(after)
    grad_refs, dlogit_refs = take(count), [take(count) for _ in range(2)]
    each = piece_refs[0].shape[0]
    if each * count <= ROWS:
        units = [[(i, 0, each) for i in range(count)]]
    else:
        rows = min(ROWS, each)
        units = [[(i, start, rows)] for i in range(count) for start in range(0, each, rows)]

    def gather(unit, refs, at=lambda i: 0):
        values = [refs[i][at(i) + start : at(i) + start + rows] for i, start, rows in unit]
        return values[0] if len(values) == 1 else jnp.concatenate(values, 0)

    for unit in units:
        block = gather(unit, piece_refs)
        grad = None
        for emb_ref, turned_ref, target_ref, out_refs in zip(emb_refs, turned_refs, target_refs, dlogit_refs):
            logits = jnp.dot(block, turned_ref[...], preferred_element_type=F32)
            signed = gather(unit, [target_ref] * count, lambda i: which[i] * each).astype(F32)
            dlogits = (signed * jax.nn.sigmoid(jnp.where(signed < 0, -logits, logits))).astype(BF16)
            term = jnp.dot(dlogits, emb_ref[...], preferred_element_type=F32)
            grad = term if grad is None else grad + term
            off = 0
            for i, start, rows in unit:
                out_refs[i][start : start + rows] = dlogits[off : off + rows]
                off += rows
        off = 0
        for i, start, rows in unit:
            grad_refs[i][start : start + rows] = grad[off : off + rows].astype(grad_refs[i].dtype)
            off += rows


def join_kernel(*refs, count):
    for k in range(3):
        out_ref = refs[3 * count + k]
        at = 0
        for ref in refs[k * count : (k + 1) * count]:
            out_ref[at : at + ref.shape[0]] = ref[...]
            at += ref.shape[0]


def emb_kernel(d_own_ref, d_other_ref, c_own_ref, c_other_ref, after_ref, out_ref):
    dims = (((0,), (0,)), ((), ()))
    out_ref[...] = lax.dot_general(
        d_own_ref[...], c_own_ref[...], dims, preferred_element_type=F32
    ) + lax.dot_general(d_other_ref[...], c_other_ref[...], dims, preferred_element_type=F32)


def finish_kernel(grad_ref, received_ref, column_ref, after_hbm, out_ref):
    out_ref[...] = (grad_ref[...] + received_ref[...].astype(F32)) * column_ref[:, :1]


def hbm(count):
    return [pl.BlockSpec(memory_space=pltpu.HBM)] * count


def vmem(count):
    return [pl.BlockSpec(memory_space=pltpu.VMEM)] * count


def keep(*arrays):
    return [pltpu.with_memory_space_constraint(x, pltpu.HBM) for x in arrays]


def cost(flops, nbytes):
    return pl.CostEstimate(flops=flops, bytes_accessed=nbytes, transcendentals=0)


def params(*sizes):
    return pltpu.CompilerParams(vmem_limit_bytes=(2 * sum(sizes) // MIB + 4) * MIB)


def shards(embeddings, classifier, label_valid, shortlist, slot_live, positive, negative):
    lab = lax.axis_size("lab")
    enc = lax.axis_size("enc")
    docs, width = embeddings.shape
    panel = classifier.shape[0]
    slots = shortlist.shape[1]
    half = lab // 2 * panel
    groups = bit_groups(lab)

    negatives = negative.shape[2]
    height = slots * (negatives + 2)
    packed, column, index_own = pl.pallas_call(
        functools.partial(pack_kernel, scale=1.0 / math.sqrt(docs * enc * slots)),
        out_shape=[
            jax.ShapeDtypeStruct((panel, width), BF16),
            jax.ShapeDtypeStruct((panel, LANES), F32),
            jax.ShapeDtypeStruct((height, docs), jnp.int32),
        ],
        in_specs=hbm(6),
        out_specs=vmem(3),
        scratch_shapes=[pltpu.VMEM((panel, width), F32), pltpu.VMEM((1, panel), jnp.int32)]
        + [pltpu.VMEM((slots, docs), jnp.int32)] * 3
        + [pltpu.SemaphoreType.DMA((5 + slots,))],
        compiler_params=params(panel * width * 6, height * docs * 4),
        cost_estimate=cost(panel * width, panel * width * 6 + height * docs * 4),
        name="pack",
    )(
        *keep(
            classifier, label_valid.reshape(1, panel), shortlist.T, slot_live.T, positive.T,
            negative.transpose(1, 2, 0),
        )
    )
    pieces = [packed]
    for group in groups:
        own = pieces[0] if len(pieces) == 1 else jnp.concatenate(pieces, 0)
        pieces = [own] + [flip(own, "lab", mask) for mask in group_masks(group)]

    emb_other = flip(embeddings, "lab", 1)
    index_other = flip(index_own, "lab", 1)
    emb_own, own_turned, other_turned = pl.pallas_call(
        turn_kernel,
        out_shape=[jax.ShapeDtypeStruct((docs, width), BF16)]
        + [jax.ShapeDtypeStruct((width, docs), BF16)] * 2,
        in_specs=hbm(1) + vmem(1),
        out_specs=vmem(3),
        scratch_shapes=[pltpu.SemaphoreType.DMA],
        compiler_params=params(docs * width * 10),
        cost_estimate=cost(docs * width, docs * width * 10),
        name="turn",
    )(*keep(embeddings), emb_other)
    target_own, target_other = pl.pallas_call(
        functools.partial(targets_kernel, panel=panel, slots=slots),
        out_shape=[jax.ShapeDtypeStruct((half, docs), BF16)] * 2,
        in_specs=vmem(3),
        out_specs=vmem(2),
        compiler_params=params(height * docs * 8, docs * half * 4),
        cost_estimate=cost(docs * panel * slots * 80, height * docs * 8 + docs * half * 4),
        name="targets",
    )(index_own, index_other, other_turned)

    each = pieces[0].shape[0]
    number = len(pieces)

    def score(which, after):
        count, rows = len(which), each * len(which)
        outs = pl.pallas_call(
            functools.partial(score_kernel, which=which, after=len(after)),
            out_shape=[jax.ShapeDtypeStruct((each, width), BF16 if i else F32) for i in which]
            + [jax.ShapeDtypeStruct((each, docs), BF16)] * (2 * count),
            in_specs=vmem(count + 6 + len(after)),
            out_specs=vmem(3 * count),
            compiler_params=params(8 * docs * width, 16 * rows * docs, 12 * rows * width),
            cost_estimate=cost(
                8 * docs * rows * width, 8 * docs * width + 8 * rows * docs + 8 * rows * width
            ),
            name="score",
        )(
            *[pieces[i] for i in which], emb_own, emb_other, own_turned, other_turned,
            target_own, target_other, *after,
        )
        return outs[:count], outs[count : 2 * count], outs[2 * count :]

    order = [number - 1, 0] + list(range(1, number - 1))
    grads, dlogits = {}, ([], [])
    for which in [w for w in (order[:2], order[2:]) if w]:
        results = score(which, list(grads.values())[:1])
        grads.update(zip(which, results[0]))
        for store, values in zip(dlogits, results[1:]):
            store += values
    classifier_own, d_own, d_theirs = pl.pallas_call(
        functools.partial(join_kernel, count=number),
        out_shape=[jax.ShapeDtypeStruct((half, width), BF16)]
        + [jax.ShapeDtypeStruct((half, docs), BF16)] * 2,
        in_specs=vmem(3 * number),
        out_specs=vmem(3),
        compiler_params=params(4 * half * width, 8 * half * docs),
        cost_estimate=cost(0, 4 * half * width + 8 * half * docs),
        name="join",
    )(*[pieces[i] for i in order], *dlogits[0], *dlogits[1])

    grad = None
    for group in reversed(groups):
        masks = group_masks(group)
        if grad is not None:
            grad = grad.reshape(len(masks) + 1, -1, width)
            grads = [grad[0]] + [grad[i].astype(BF16) for i in range(1, len(masks) + 1)]
        received = []
        for i in reversed(range(len(masks))):
            value = grads[i + 1]
            if i == 2:
                value = jnp.concatenate([value, value[:16]], 0)
            received.append(flip(value, "lab", masks[i])[: grads[i + 1].shape[0]])
        grad = grads[0]
        for r in received:
            grad = grad + r.astype(F32)
    if grad is None:
        grad = grads[0]
    d_other, classifier_other = flip(d_theirs, "lab", 1), flip(classifier_own, "lab", 1)
    bits = [1 << bit for bit in range(enc.bit_length() - 1)]
    for bit in bits[:-1]:
        grad = grad + flip(grad.astype(BF16), "enc", bit).astype(F32)
    received = flip(grad.astype(BF16), "enc", bits[-1])

    emb_grad = pl.pallas_call(
        emb_kernel,
        out_shape=jax.ShapeDtypeStruct((docs, width), F32),
        in_specs=vmem(5),
        out_specs=pl.BlockSpec(memory_space=pltpu.VMEM),
        compiler_params=params(8 * docs * width, 4 * half * docs, 4 * half * width),
        cost_estimate=cost(4 * docs * half * width, 4 * docs * width + 4 * half * docs + 4 * half * width),
        name="emb_grad",
    )(d_own, d_other, classifier_own, classifier_other, grad)

    w_grad = pl.pallas_call(
        finish_kernel,
        out_shape=jax.ShapeDtypeStruct((panel, width), F32),
        in_specs=vmem(3) + hbm(1),
        out_specs=pl.BlockSpec(memory_space=pltpu.VMEM),
        compiler_params=params(panel * width * 10),
        cost_estimate=cost(panel * width, panel * width * 10),
        name="finish",
    )(grad, received, column, *keep(emb_grad))
    return (w_grad, emb_grad)


def solution(mesh):
    in_specs = (
        P(("enc", "lab"), None),
        P("lab", None),
        P("lab"),
        P(("enc", "lab"), None),
        P(("enc", "lab"), None),
        P(("enc", "lab"), None),
        P(("enc", "lab"), None, None),
    )
    out_specs = (P("lab", None), P(("enc", "lab"), None))
    return jax.shard_map(shards, mesh=mesh, in_specs=in_specs, out_specs=out_specs, check_vma=False)
```

```python
import functools
import math

import jax
import jax.numpy as jnp
from jax import lax
from jax.experimental import pallas as pl
from jax.experimental.pallas import tpu as pltpu
from jax.sharding import PartitionSpec as P

BF16 = jnp.bfloat16
F32 = jnp.float32
LANES = 128
PACKED = 16
ROWS = 256
MIB = 1024 * 1024


def flip(value, axis, mask):
    return lax.ppermute(value, axis, [(i, i ^ mask) for i in range(lax.axis_size(axis))])


def bit_groups(count):
    masks = [1 << b for b in range(1, count.bit_length() - 1)]
    return [tuple(masks[i : i + 2]) for i in range(0, len(masks), 2)]


def group_masks(group):
    return [group[0]] if len(group) == 1 else [group[0], group[1], group[0] | group[1]]


def fetch(sources, targets, sem):
    copies = [pltpu.make_async_copy(x, y, sem.at[i]) for i, (x, y) in enumerate(zip(sources, targets))]
    for copy in copies:
        copy.start()
    for copy in copies:
        copy.wait()


def flag_column(flags):
    panel = flags.shape[1]
    diagonal = lax.broadcasted_iota(jnp.int32, (panel, panel), 0) == lax.broadcasted_iota(
        jnp.int32, (panel, panel), 1
    )
    spread = jnp.broadcast_to(flags.astype(F32), (panel, panel))
    return jnp.sum(jnp.where(diagonal, spread, 0.0), axis=1, keepdims=True)


def pack_kernel(
    classifier_hbm, valid_hbm, short_hbm, live_hbm, pos_hbm, neg_hbm, rows_ref, column_ref, index_ref,
    classifier_ref, valid_ref, short_ref, live_ref, pos_ref, neg_ref, sem, *, scale
):
    slots, negatives, docs = neg_ref.shape
    fetch(
        (classifier_hbm, valid_hbm, short_hbm, live_hbm, pos_hbm, neg_hbm),
        (classifier_ref, valid_ref, short_ref, live_ref, pos_ref, neg_ref),
        sem,
    )
    column = flag_column(valid_ref[...])
    rows_ref[...] = (classifier_ref[...] * column).astype(BF16)
    column_ref[...] = jnp.broadcast_to(column * scale, column_ref.shape)
    index_ref[...] = jnp.concatenate(
        [
            neg_ref[...].reshape(slots * negatives, docs),
            pos_ref[...],
            jnp.where(live_ref[...] > 0, short_ref[...], -1),
        ],
        0,
    ).astype(F32).astype(BF16)


def turn_kernel(emb_hbm, other_ref, own_ref, own_turned_ref, other_turned_ref, sem):
    copy = pltpu.make_async_copy(emb_hbm, own_ref, sem)
    copy.start()
    other_turned_ref[...] = other_ref[...].T
    copy.wait()
    own_turned_ref[...] = own_ref[...].T


def targets_kernel(index_own_ref, index_other_ref, after_ref, target_own_ref, target_other_ref, *, panel, slots):
    me = lax.axis_index("lab")
    docs = index_own_ref.shape[1]
    negatives = index_own_ref.shape[0] // slots - 2
    shape = (panel // PACKED, PACKED, LANES)
    label = PACKED * lax.broadcasted_iota(jnp.int32, shape, 0) + lax.broadcasted_iota(jnp.int32, shape, 1)
    label = label.astype(F32).astype(BF16)
    one, zero = jnp.ones((), BF16), jnp.zeros((), BF16)

    def fill(index_ref, out_ref, lanes):
        index = index_ref[:, lanes].astype(F32)

        def row(at):
            return jnp.broadcast_to(index[at : at + 1], (PACKED, LANES))

        values, relative = [], []
        for s in range(slots):
            count = jnp.zeros(shape, BF16)
            for k in range(negatives):
                count = count + jnp.where(row(s * negatives + k).astype(BF16)[None] == label, one, zero)
            hot = row(slots * negatives + s).astype(BF16)[None] == label
            values.append(jnp.where(hot, -one - count, count))
            relative.append(row(slots * (negatives + 1) + s).astype(jnp.int32) ^ me)
        for j in range(out_ref.shape[0] // panel):
            block = jnp.zeros(shape, BF16)
            for s in range(slots):
                chosen = jnp.where(relative[s] == 2 * j, 1.0, 0.0).astype(BF16)
                block = block + chosen[None] * values[s]
            out_ref[pl.ds(j * panel, panel), lanes] = block.reshape(panel, LANES)

    def chunk(i, carry):
        lanes = pl.ds(pl.multiple_of(i * LANES, LANES), LANES)
        fill(index_own_ref, target_own_ref, lanes)
        fill(index_other_ref, target_other_ref, lanes)
        return carry

    lax.fori_loop(0, docs // LANES, chunk, 0)


def score_kernel(*refs, which, after):
    refs = list(refs)

    def take(number):
        return [refs.pop(0) for _ in range(number)]

    count = len(which)
    piece_refs, emb_refs, turned_refs, target_refs = take(count), take(2), take(2), take(2)
    take(after)
    grad_refs, dlogit_refs = take(count), [take(count) for _ in range(2)]
    each = piece_refs[0].shape[0]
    if each * count <= ROWS:
        units = [[(i, 0, each) for i in range(count)]]
    else:
        rows = min(ROWS, each)
        units = [[(i, start, rows)] for i in range(count) for start in range(0, each, rows)]

    def gather(unit, refs, at=lambda i: 0):
        values = [refs[i][at(i) + start : at(i) + start + rows] for i, start, rows in unit]
        return values[0] if len(values) == 1 else jnp.concatenate(values, 0)

    for unit in units:
        block = gather(unit, piece_refs)
        grad = None
        for emb_ref, turned_ref, target_ref, out_refs in zip(emb_refs, turned_refs, target_refs, dlogit_refs):
            logits = jnp.dot(block, turned_ref[...], preferred_element_type=F32)
            signed = gather(unit, [target_ref] * count, lambda i: which[i] * each).astype(F32)
            dlogits = (signed * jax.nn.sigmoid(jnp.where(signed < 0, -logits, logits))).astype(BF16)
            term = jnp.dot(dlogits, emb_ref[...], preferred_element_type=F32)
            grad = term if grad is None else grad + term
            off = 0
            for i, start, rows in unit:
                out_refs[i][start : start + rows] = dlogits[off : off + rows]
                off += rows
        off = 0
        for i, start, rows in unit:
            grad_refs[i][start : start + rows] = grad[off : off + rows].astype(grad_refs[i].dtype)
            off += rows


def join_kernel(*refs, count):
    for k in range(3):
        out_ref = refs[3 * count + k]
        at = 0
        for ref in refs[k * count : (k + 1) * count]:
            out_ref[at : at + ref.shape[0]] = ref[...]
            at += ref.shape[0]


def emb_kernel(d_own_ref, d_other_ref, c_own_ref, c_other_ref, after_ref, out_ref):
    dims = (((0,), (0,)), ((), ()))
    out_ref[...] = lax.dot_general(
        d_own_ref[...], c_own_ref[...], dims, preferred_element_type=F32
    ) + lax.dot_general(d_other_ref[...], c_other_ref[...], dims, preferred_element_type=F32)


def finish_kernel(grad_ref, received_ref, column_ref, after_hbm, out_ref):
    out_ref[...] = (grad_ref[...] + received_ref[...].astype(F32)) * column_ref[:, :1]


def hbm(count):
    return [pl.BlockSpec(memory_space=pltpu.HBM)] * count


def vmem(count):
    return [pl.BlockSpec(memory_space=pltpu.VMEM)] * count


def keep(*arrays):
    return [pltpu.with_memory_space_constraint(x, pltpu.HBM) for x in arrays]


def cost(flops, nbytes):
    return pl.CostEstimate(flops=flops, bytes_accessed=nbytes, transcendentals=0)


def params(*sizes):
    return pltpu.CompilerParams(vmem_limit_bytes=(2 * sum(sizes) // MIB + 4) * MIB)


def shards(embeddings, classifier, label_valid, shortlist, slot_live, positive, negative):
    lab = lax.axis_size("lab")
    enc = lax.axis_size("enc")
    docs, width = embeddings.shape
    panel = classifier.shape[0]
    slots = shortlist.shape[1]
    half = lab // 2 * panel
    groups = bit_groups(lab)

    negatives = negative.shape[2]
    height = slots * (negatives + 2)
    packed, column, index_own = pl.pallas_call(
        functools.partial(pack_kernel, scale=1.0 / math.sqrt(docs * enc * slots)),
        out_shape=[
            jax.ShapeDtypeStruct((panel, width), BF16),
            jax.ShapeDtypeStruct((panel, LANES), F32),
            jax.ShapeDtypeStruct((height, docs), BF16),
        ],
        in_specs=hbm(6),
        out_specs=vmem(3),
        scratch_shapes=[pltpu.VMEM((panel, width), F32), pltpu.VMEM((1, panel), jnp.int32)]
        + [pltpu.VMEM((slots, docs), jnp.int32)] * 3
        + [pltpu.VMEM((slots, negatives, docs), jnp.int32), pltpu.SemaphoreType.DMA((6,))],
        compiler_params=params(panel * width * 6, height * docs * 4),
        cost_estimate=cost(panel * width, panel * width * 6 + height * docs * 4),
        name="pack",
    )(
        *keep(
            classifier, label_valid.reshape(1, panel), shortlist.T, slot_live.T, positive.T,
            negative.transpose(1, 2, 0),
        )
    )
    pieces = [packed]
    for group in groups:
        own = pieces[0] if len(pieces) == 1 else jnp.concatenate(pieces, 0)
        pieces = [own] + [flip(own, "lab", mask) for mask in group_masks(group)]

    emb_other = flip(embeddings, "lab", 1)
    index_other = flip(index_own, "lab", 1)
    emb_own, own_turned, other_turned = pl.pallas_call(
        turn_kernel,
        out_shape=[jax.ShapeDtypeStruct((docs, width), BF16)]
        + [jax.ShapeDtypeStruct((width, docs), BF16)] * 2,
        in_specs=hbm(1) + vmem(1),
        out_specs=vmem(3),
        scratch_shapes=[pltpu.SemaphoreType.DMA],
        compiler_params=params(docs * width * 10),
        cost_estimate=cost(docs * width, docs * width * 10),
        name="turn",
    )(*keep(embeddings), emb_other)
    target_own, target_other = pl.pallas_call(
        functools.partial(targets_kernel, panel=panel, slots=slots),
        out_shape=[jax.ShapeDtypeStruct((half, docs), BF16)] * 2,
        in_specs=vmem(3),
        out_specs=vmem(2),
        compiler_params=params(height * docs * 8, docs * half * 4),
        cost_estimate=cost(docs * panel * slots * 80, height * docs * 8 + docs * half * 4),
        name="targets",
    )(index_own, index_other, other_turned)

    each = pieces[0].shape[0]
    number = len(pieces)

    def score(which, after):
        count, rows = len(which), each * len(which)
        outs = pl.pallas_call(
            functools.partial(score_kernel, which=which, after=len(after)),
            out_shape=[jax.ShapeDtypeStruct((each, width), BF16 if i else F32) for i in which]
            + [jax.ShapeDtypeStruct((each, docs), BF16)] * (2 * count),
            in_specs=vmem(count + 6 + len(after)),
            out_specs=vmem(3 * count),
            compiler_params=params(8 * docs * width, 16 * rows * docs, 12 * rows * width),
            cost_estimate=cost(
                8 * docs * rows * width, 8 * docs * width + 8 * rows * docs + 8 * rows * width
            ),
            name="score",
        )(
            *[pieces[i] for i in which], emb_own, emb_other, own_turned, other_turned,
            target_own, target_other, *after,
        )
        return outs[:count], outs[count : 2 * count], outs[2 * count :]

    order = [number - 1, 0] + list(range(1, number - 1))
    grads, dlogits = {}, ([], [])
    for which in [w for w in (order[:2], order[2:]) if w]:
        results = score(which, list(grads.values())[:1])
        grads.update(zip(which, results[0]))
        for store, values in zip(dlogits, results[1:]):
            store += values
    classifier_own, d_own, d_theirs = pl.pallas_call(
        functools.partial(join_kernel, count=number),
        out_shape=[jax.ShapeDtypeStruct((half, width), BF16)]
        + [jax.ShapeDtypeStruct((half, docs), BF16)] * 2,
        in_specs=vmem(3 * number),
        out_specs=vmem(3),
        compiler_params=params(4 * half * width, 8 * half * docs),
        cost_estimate=cost(0, 4 * half * width + 8 * half * docs),
        name="join",
    )(*[pieces[i] for i in order], *dlogits[0], *dlogits[1])

    grad = None
    for group in reversed(groups):
        masks = group_masks(group)
        if grad is not None:
            grad = grad.reshape(len(masks) + 1, -1, width)
            grads = [grad[0]] + [grad[i].astype(BF16) for i in range(1, len(masks) + 1)]
        received = []
        for i in reversed(range(len(masks))):
            value = grads[i + 1]
            if i == 2:
                value = jnp.concatenate([value, value[:16]], 0)
            received.append(flip(value, "lab", masks[i])[: grads[i + 1].shape[0]])
        grad = grads[0]
        for r in received:
            grad = grad + r.astype(F32)
    if grad is None:
        grad = grads[0]
    d_other, classifier_other = flip(d_theirs, "lab", 1), flip(classifier_own, "lab", 1)
    bits = [1 << bit for bit in range(enc.bit_length() - 1)]
    for bit in bits[:-1]:
        grad = grad + flip(grad.astype(BF16), "enc", bit).astype(F32)
    received = flip(grad.astype(BF16), "enc", bits[-1])

    emb_grad = pl.pallas_call(
        emb_kernel,
        out_shape=jax.ShapeDtypeStruct((docs, width), F32),
        in_specs=vmem(5),
        out_specs=pl.BlockSpec(memory_space=pltpu.VMEM),
        compiler_params=params(8 * docs * width, 4 * half * docs, 4 * half * width),
        cost_estimate=cost(4 * docs * half * width, 4 * docs * width + 4 * half * docs + 4 * half * width),
        name="emb_grad",
    )(d_own, d_other, classifier_own, classifier_other, grad)

    w_grad = pl.pallas_call(
        finish_kernel,
        out_shape=jax.ShapeDtypeStruct((panel, width), F32),
        in_specs=vmem(3) + hbm(1),
        out_specs=pl.BlockSpec(memory_space=pltpu.VMEM),
        compiler_params=params(panel * width * 10),
        cost_estimate=cost(panel * width, panel * width * 10),
        name="finish",
    )(grad, received, column, *keep(emb_grad))
    return (w_grad, emb_grad)


def solution(mesh):
    in_specs = (
        P(("enc", "lab"), None),
        P("lab", None),
        P("lab"),
        P(("enc", "lab"), None),
        P(("enc", "lab"), None),
        P(("enc", "lab"), None),
        P(("enc", "lab"), None, None),
    )
    out_specs = (P("lab", None), P(("enc", "lab"), None))
    return jax.shard_map(shards, mesh=mesh, in_specs=in_specs, out_specs=out_specs, check_vma=False)
```

```python
import functools
import math

import jax
import jax.numpy as jnp
from jax import lax
from jax.experimental import pallas as pl
from jax.experimental.pallas import tpu as pltpu
from jax.sharding import PartitionSpec as P

BF16 = jnp.bfloat16
F32 = jnp.float32
LANES = 128
PACKED = 16
ROWS = 256
MIB = 1024 * 1024


def flip(value, axis, mask):
    return lax.ppermute(value, axis, [(i, i ^ mask) for i in range(lax.axis_size(axis))])


def bit_groups(count):
    masks = [1 << b for b in range(1, count.bit_length() - 1)]
    return [tuple(masks[i : i + 2]) for i in range(0, len(masks), 2)]


def group_masks(group):
    return [group[0]] if len(group) == 1 else [group[0], group[1], group[0] | group[1]]


def fetch(sources, targets, sem):
    copies = [pltpu.make_async_copy(x, y, sem.at[i]) for i, (x, y) in enumerate(zip(sources, targets))]
    for copy in copies:
        copy.start()
    for copy in copies:
        copy.wait()


def flag_column(flags):
    panel = flags.shape[1]
    diagonal = lax.broadcasted_iota(jnp.int32, (panel, panel), 0) == lax.broadcasted_iota(
        jnp.int32, (panel, panel), 1
    )
    spread = jnp.broadcast_to(flags.astype(F32), (panel, panel))
    return jnp.sum(jnp.where(diagonal, spread, 0.0), axis=1, keepdims=True)


def pack_kernel(
    classifier_hbm, valid_hbm, short_hbm, live_hbm, pos_hbm, neg_hbm, rows_ref, column_ref, index_ref,
    classifier_ref, valid_ref, short_ref, live_ref, pos_ref, neg_ref, sem, *, scale
):
    slots, negatives, docs = neg_ref.shape
    fetch(
        (classifier_hbm, valid_hbm, short_hbm, live_hbm, pos_hbm, neg_hbm),
        (classifier_ref, valid_ref, short_ref, live_ref, pos_ref, neg_ref),
        sem,
    )
    column = flag_column(valid_ref[...])
    rows_ref[...] = (classifier_ref[...] * column).astype(BF16)
    column_ref[...] = jnp.broadcast_to(column * scale, column_ref.shape)
    index_ref[...] = jnp.concatenate(
        [
            neg_ref[...].reshape(slots * negatives, docs),
            pos_ref[...],
            jnp.where(live_ref[...] > 0, short_ref[...], -1),
        ],
        0,
    ).astype(F32).astype(BF16)


def turn_kernel(emb_hbm, other_ref, own_ref, own_turned_ref, other_turned_ref, sem):
    copy = pltpu.make_async_copy(emb_hbm, own_ref, sem)
    copy.start()
    other_turned_ref[...] = other_ref[...].T
    copy.wait()
    own_turned_ref[...] = own_ref[...].T


def targets_kernel(index_own_ref, index_other_ref, after_ref, target_own_ref, target_other_ref, *, panel, slots):
    me = lax.axis_index("lab")
    docs = index_own_ref.shape[1]
    negatives = index_own_ref.shape[0] // slots - 2
    shape = (panel // PACKED, PACKED, LANES)
    label = PACKED * lax.broadcasted_iota(jnp.int32, shape, 0) + lax.broadcasted_iota(jnp.int32, shape, 1)
    label = label.astype(F32).astype(BF16)
    one, zero = jnp.ones((), BF16), jnp.zeros((), BF16)

    def fill(index_ref, out_ref, lanes):
        index = index_ref[:, lanes].astype(F32)

        def row(at):
            return jnp.broadcast_to(index[at : at + 1], (PACKED, LANES))

        values, relative = [], []
        for s in range(slots):
            count = jnp.zeros(shape, BF16)
            for k in range(negatives):
                count = count + jnp.where(row(s * negatives + k).astype(BF16)[None] == label, one, zero)
            hot = row(slots * negatives + s).astype(BF16)[None] == label
            values.append(jnp.where(hot, -one - count, count))
            relative.append(row(slots * (negatives + 1) + s).astype(jnp.int32) ^ me)
        for j in range(out_ref.shape[0] // panel):
            block = jnp.zeros(shape, BF16)
            for s in range(slots):
                chosen = jnp.where(relative[s] == 2 * j, 1.0, 0.0).astype(BF16)
                block = block + chosen[None] * values[s]
            out_ref[pl.ds(j * panel, panel), lanes] = block.reshape(panel, LANES)

    def chunk(i, carry):
        lanes = pl.ds(pl.multiple_of(i * LANES, LANES), LANES)
        fill(index_own_ref, target_own_ref, lanes)
        fill(index_other_ref, target_other_ref, lanes)
        return carry

    lax.fori_loop(0, docs // LANES, chunk, 0)


def score_kernel(*refs, which, after):
    refs = list(refs)

    def take(number):
        return [refs.pop(0) for _ in range(number)]

    count = len(which)
    piece_refs, emb_refs, turned_refs, target_refs = take(count), take(2), take(2), take(2)
    take(after)
    grad_refs, dlogit_refs = take(count), [take(count) for _ in range(2)]
    each = piece_refs[0].shape[0]
    if each * count <= ROWS:
        units = [[(i, 0, each) for i in range(count)]]
    else:
        rows = min(ROWS, each)
        units = [[(i, start, rows)] for i in range(count) for start in range(0, each, rows)]

    def gather(unit, refs, at=lambda i: 0):
        values = [refs[i][at(i) + start : at(i) + start + rows] for i, start, rows in unit]
        return values[0] if len(values) == 1 else jnp.concatenate(values, 0)

    for unit in units:
        block = gather(unit, piece_refs)
        grad = None
        for emb_ref, turned_ref, target_ref, out_refs in zip(emb_refs, turned_refs, target_refs, dlogit_refs):
            logits = jnp.dot(block, turned_ref[...], preferred_element_type=F32)
            signed = gather(unit, [target_ref] * count, lambda i: which[i] * each).astype(F32)
            dlogits = (signed * jax.nn.sigmoid(jnp.where(signed < 0, -logits, logits))).astype(BF16)
            term = jnp.dot(dlogits, emb_ref[...], preferred_element_type=F32)
            grad = term if grad is None else grad + term
            off = 0
            for i, start, rows in unit:
                out_refs[i][start : start + rows] = dlogits[off : off + rows]
                off += rows
        off = 0
        for i, start, rows in unit:
            grad_refs[i][start : start + rows] = grad[off : off + rows].astype(grad_refs[i].dtype)
            off += rows


def join_kernel(*refs, count):
    for k in range(3):
        out_ref = refs[3 * count + k]
        at = 0
        for ref in refs[k * count : (k + 1) * count]:
            out_ref[at : at + ref.shape[0]] = ref[...]
            at += ref.shape[0]


def emb_kernel(d_own_ref, d_other_ref, c_own_ref, c_other_ref, after_ref, out_ref):
    dims = (((0,), (0,)), ((), ()))
    out_ref[...] = lax.dot_general(
        d_own_ref[...], c_own_ref[...], dims, preferred_element_type=F32
    ) + lax.dot_general(d_other_ref[...], c_other_ref[...], dims, preferred_element_type=F32)


def finish_kernel(grad_ref, received_ref, column_ref, after_hbm, out_ref):
    out_ref[...] = (grad_ref[...] + received_ref[...].astype(F32)) * column_ref[:, :1]


def hbm(count):
    return [pl.BlockSpec(memory_space=pltpu.HBM)] * count


def vmem(count):
    return [pl.BlockSpec(memory_space=pltpu.VMEM)] * count


def keep(*arrays):
    return [pltpu.with_memory_space_constraint(x, pltpu.HBM) for x in arrays]


def cost(flops, nbytes):
    return pl.CostEstimate(flops=flops, bytes_accessed=nbytes, transcendentals=0)


def params(*sizes):
    return pltpu.CompilerParams(vmem_limit_bytes=(2 * sum(sizes) // MIB + 4) * MIB)


def shards(embeddings, classifier, label_valid, shortlist, slot_live, positive, negative):
    lab = lax.axis_size("lab")
    enc = lax.axis_size("enc")
    docs, width = embeddings.shape
    panel = classifier.shape[0]
    slots = shortlist.shape[1]
    half = lab // 2 * panel
    groups = bit_groups(lab)

    negatives = negative.shape[2]
    height = slots * (negatives + 2)
    packed, column, index_own = pl.pallas_call(
        functools.partial(pack_kernel, scale=1.0 / math.sqrt(docs * enc * slots)),
        out_shape=[
            jax.ShapeDtypeStruct((panel, width), BF16),
            jax.ShapeDtypeStruct((panel, LANES), F32),
            jax.ShapeDtypeStruct((height, docs), BF16),
        ],
        in_specs=hbm(6),
        out_specs=vmem(3),
        scratch_shapes=[pltpu.VMEM((panel, width), F32), pltpu.VMEM((1, panel), jnp.int32)]
        + [pltpu.VMEM((slots, docs), jnp.int32)] * 3
        + [pltpu.VMEM((slots, negatives, docs), jnp.int32), pltpu.SemaphoreType.DMA((6,))],
        compiler_params=params(panel * width * 6, height * docs * 4),
        cost_estimate=cost(panel * width, panel * width * 6 + height * docs * 4),
        name="pack",
    )(
        *keep(
            classifier, label_valid.reshape(1, panel), shortlist.T, slot_live.T, positive.T,
            negative.transpose(1, 2, 0),
        )
    )
    pieces = [packed]
    for group in groups:
        own = pieces[0] if len(pieces) == 1 else jnp.concatenate(pieces, 0)
        pieces = [own] + [flip(own, "lab", mask) for mask in group_masks(group)]

    emb_other = flip(embeddings, "lab", 1)
    index_other = flip(index_own, "lab", 1)
    emb_own, own_turned, other_turned = pl.pallas_call(
        turn_kernel,
        out_shape=[jax.ShapeDtypeStruct((docs, width), BF16)]
        + [jax.ShapeDtypeStruct((width, docs), BF16)] * 2,
        in_specs=hbm(1) + vmem(1),
        out_specs=vmem(3),
        scratch_shapes=[pltpu.SemaphoreType.DMA],
        compiler_params=params(docs * width * 10),
        cost_estimate=cost(docs * width, docs * width * 10),
        name="turn",
    )(*keep(embeddings), emb_other)
    target_own, target_other = pl.pallas_call(
        functools.partial(targets_kernel, panel=panel, slots=slots),
        out_shape=[jax.ShapeDtypeStruct((half, docs), BF16)] * 2,
        in_specs=vmem(3),
        out_specs=vmem(2),
        compiler_params=params(height * docs * 8, docs * half * 4),
        cost_estimate=cost(docs * panel * slots * 80, height * docs * 8 + docs * half * 4),
        name="targets",
    )(index_own, index_other, other_turned)

    each = pieces[0].shape[0]
    number = len(pieces)

    def score(which, after):
        count, rows = len(which), each * len(which)
        outs = pl.pallas_call(
            functools.partial(score_kernel, which=which, after=len(after)),
            out_shape=[jax.ShapeDtypeStruct((each, width), BF16 if i else F32) for i in which]
            + [jax.ShapeDtypeStruct((each, docs), BF16)] * (2 * count),
            in_specs=vmem(count + 6 + len(after)),
            out_specs=vmem(3 * count),
            compiler_params=params(8 * docs * width, 16 * rows * docs, 12 * rows * width),
            cost_estimate=cost(
                8 * docs * rows * width, 8 * docs * width + 8 * rows * docs + 8 * rows * width
            ),
            name="score",
        )(
            *[pieces[i] for i in which], emb_own, emb_other, own_turned, other_turned,
            target_own, target_other, *after,
        )
        return outs[:count], outs[count : 2 * count], outs[2 * count :]

    order = [number - 1, 0] + list(range(1, number - 1))
    grads, dlogits = {}, ([], [])
    for which in [w for w in (order[:2], order[2:]) if w]:
        results = score(which, list(grads.values())[:1])
        grads.update(zip(which, results[0]))
        for store, values in zip(dlogits, results[1:]):
            store += values
    classifier_own, d_own, d_theirs = pl.pallas_call(
        functools.partial(join_kernel, count=number),
        out_shape=[jax.ShapeDtypeStruct((half, width), BF16)]
        + [jax.ShapeDtypeStruct((half, docs), BF16)] * 2,
        in_specs=vmem(3 * number),
        out_specs=vmem(3),
        compiler_params=params(4 * half * width, 8 * half * docs),
        cost_estimate=cost(0, 4 * half * width + 8 * half * docs),
        name="join",
    )(*[pieces[i] for i in order], *dlogits[0], *dlogits[1])

    grad = None
    for group in reversed(groups):
        masks = group_masks(group)
        if grad is not None:
            grad = grad.reshape(len(masks) + 1, -1, width)
            grads = [grad[0]] + [grad[i].astype(BF16) for i in range(1, len(masks) + 1)]
        received = []
        for i in reversed(range(len(masks))):
            value = grads[i + 1]
            if i == 2:
                value = jnp.concatenate([value, value[:1]], 0)
            received.append(flip(value, "lab", masks[i])[: grads[i + 1].shape[0]])
        grad = grads[0]
        for r in received:
            grad = grad + r.astype(F32)
    if grad is None:
        grad = grads[0]
    d_other, classifier_other = flip(d_theirs, "lab", 1), flip(classifier_own, "lab", 1)
    bits = [1 << bit for bit in range(enc.bit_length() - 1)]
    for bit in bits[:-1]:
        grad = grad + flip(grad.astype(BF16), "enc", bit).astype(F32)
    received = flip(grad.astype(BF16), "enc", bits[-1])

    emb_grad = pl.pallas_call(
        emb_kernel,
        out_shape=jax.ShapeDtypeStruct((docs, width), F32),
        in_specs=vmem(5),
        out_specs=pl.BlockSpec(memory_space=pltpu.VMEM),
        compiler_params=params(8 * docs * width, 4 * half * docs, 4 * half * width),
        cost_estimate=cost(4 * docs * half * width, 4 * docs * width + 4 * half * docs + 4 * half * width),
        name="emb_grad",
    )(d_own, d_other, classifier_own, classifier_other, grad)

    w_grad = pl.pallas_call(
        finish_kernel,
        out_shape=jax.ShapeDtypeStruct((panel, width), F32),
        in_specs=vmem(3) + hbm(1),
        out_specs=pl.BlockSpec(memory_space=pltpu.VMEM),
        compiler_params=params(panel * width * 10),
        cost_estimate=cost(panel * width, panel * width * 10),
        name="finish",
    )(grad, received, column, *keep(emb_grad))
    return (w_grad, emb_grad)


def solution(mesh):
    in_specs = (
        P(("enc", "lab"), None),
        P("lab", None),
        P("lab"),
        P(("enc", "lab"), None),
        P(("enc", "lab"), None),
        P(("enc", "lab"), None),
        P(("enc", "lab"), None, None),
    )
    out_specs = (P("lab", None), P(("enc", "lab"), None))
    return jax.shard_map(shards, mesh=mesh, in_specs=in_specs, out_specs=out_specs, check_vma=False)
```

```python
import functools
import math

import jax
import jax.numpy as jnp
from jax import lax
from jax.experimental import pallas as pl
from jax.experimental.pallas import tpu as pltpu
from jax.sharding import PartitionSpec as P

BF16 = jnp.bfloat16
F32 = jnp.float32
LANES = 128
PACKED = 16
ROWS = 256
MIB = 1024 * 1024


def flip(value, axis, mask):
    return lax.ppermute(value, axis, [(i, i ^ mask) for i in range(lax.axis_size(axis))])


def bit_groups(count):
    masks = [1 << b for b in range(1, count.bit_length() - 1)]
    return [tuple(masks[i : i + 2]) for i in range(0, len(masks), 2)]


def group_masks(group):
    return [group[0]] if len(group) == 1 else [group[0], group[1], group[0] | group[1]]


def fetch(sources, targets, sem):
    copies = [pltpu.make_async_copy(x, y, sem.at[i]) for i, (x, y) in enumerate(zip(sources, targets))]
    for copy in copies:
        copy.start()
    for copy in copies:
        copy.wait()


def flag_column(flags):
    panel = flags.shape[1]
    diagonal = lax.broadcasted_iota(jnp.int32, (panel, panel), 0) == lax.broadcasted_iota(
        jnp.int32, (panel, panel), 1
    )
    spread = jnp.broadcast_to(flags.astype(F32), (panel, panel))
    return jnp.sum(jnp.where(diagonal, spread, 0.0), axis=1, keepdims=True)


def pack_kernel(
    classifier_hbm, valid_hbm, short_hbm, live_hbm, pos_hbm, neg_hbm, rows_ref, column_ref, index_ref,
    classifier_ref, valid_ref, short_ref, live_ref, pos_ref, neg_ref, sem, *, scale
):
    slots, negatives, docs = neg_ref.shape
    fetch(
        (classifier_hbm, valid_hbm, short_hbm, live_hbm, pos_hbm, neg_hbm),
        (classifier_ref, valid_ref, short_ref, live_ref, pos_ref, neg_ref),
        sem,
    )
    column = flag_column(valid_ref[...])
    rows_ref[...] = (classifier_ref[...] * column).astype(BF16)
    column_ref[...] = jnp.broadcast_to(column * scale, column_ref.shape)
    index_ref[...] = jnp.concatenate(
        [
            neg_ref[...].reshape(slots * negatives, docs),
            pos_ref[...],
            jnp.where(live_ref[...] > 0, short_ref[...], -1),
        ],
        0,
    ).astype(F32).astype(BF16)


def turn_kernel(emb_hbm, other_ref, own_ref, own_turned_ref, other_turned_ref, sem):
    copy = pltpu.make_async_copy(emb_hbm, own_ref, sem)
    copy.start()
    other_turned_ref[...] = other_ref[...].T
    copy.wait()
    own_turned_ref[...] = own_ref[...].T


def targets_kernel(index_own_ref, index_other_ref, after_ref, target_own_ref, target_other_ref, *, panel, slots):
    me = lax.axis_index("lab")
    docs = index_own_ref.shape[1]
    negatives = index_own_ref.shape[0] // slots - 2
    shape = (panel // PACKED, PACKED, LANES)
    label = PACKED * lax.broadcasted_iota(jnp.int32, shape, 0) + lax.broadcasted_iota(jnp.int32, shape, 1)
    label = label.astype(F32).astype(BF16)
    one, zero = jnp.ones((), BF16), jnp.zeros((), BF16)

    def fill(index_ref, out_ref, lanes):
        index = index_ref[:, lanes].astype(F32)

        def row(at):
            return jnp.broadcast_to(index[at : at + 1], (PACKED, LANES))

        values, relative = [], []
        for s in range(slots):
            count = jnp.zeros(shape, BF16)
            for k in range(negatives):
                count = count + jnp.where(row(s * negatives + k).astype(BF16)[None] == label, one, zero)
            hot = row(slots * negatives + s).astype(BF16)[None] == label
            values.append(jnp.where(hot, -one - count, count))
            relative.append(row(slots * (negatives + 1) + s).astype(jnp.int32) ^ me)
        for j in range(out_ref.shape[0] // panel):
            block = jnp.zeros(shape, BF16)
            for s in range(slots):
                chosen = jnp.where(relative[s] == 2 * j, 1.0, 0.0).astype(BF16)
                block = block + chosen[None] * values[s]
            out_ref[pl.ds(j * panel, panel), lanes] = block.reshape(panel, LANES)

    def chunk(i, carry):
        lanes = pl.ds(pl.multiple_of(i * LANES, LANES), LANES)
        fill(index_own_ref, target_own_ref, lanes)
        fill(index_other_ref, target_other_ref, lanes)
        return carry

    lax.fori_loop(0, docs // LANES, chunk, 0)


def score_kernel(*refs, which, after):
    refs = list(refs)

    def take(number):
        return [refs.pop(0) for _ in range(number)]

    count = len(which)
    piece_refs, emb_refs, turned_refs, target_refs = take(count), take(2), take(2), take(2)
    take(after)
    grad_refs, dlogit_refs = take(count), [take(count) for _ in range(2)]
    each = piece_refs[0].shape[0]
    if each * count <= ROWS:
        units = [[(i, 0, each) for i in range(count)]]
    else:
        rows = min(ROWS, each)
        units = [[(i, start, rows)] for i in range(count) for start in range(0, each, rows)]

    def gather(unit, refs, at=lambda i: 0):
        values = [refs[i][at(i) + start : at(i) + start + rows] for i, start, rows in unit]
        return values[0] if len(values) == 1 else jnp.concatenate(values, 0)

    for unit in units:
        block = gather(unit, piece_refs)
        logits = [jnp.dot(block, ref[...], preferred_element_type=F32) for ref in turned_refs]
        dlogits = []
        for x, target_ref in zip(logits, target_refs):
            signed = gather(unit, [target_ref] * count, lambda i: which[i] * each).astype(F32)
            dlogits.append((signed * jax.nn.sigmoid(jnp.where(signed < 0, -x, x))).astype(BF16))
        grad = jnp.dot(
            jnp.concatenate(dlogits, 1),
            jnp.concatenate([ref[...] for ref in emb_refs], 0),
            preferred_element_type=F32,
        )
        off = 0
        for i, start, rows in unit:
            for d, out_refs in zip(dlogits, dlogit_refs):
                out_refs[i][start : start + rows] = d[off : off + rows]
            grad_refs[i][start : start + rows] = grad[off : off + rows].astype(grad_refs[i].dtype)
            off += rows


def join_kernel(*refs, count):
    for k in range(3):
        out_ref = refs[3 * count + k]
        at = 0
        for ref in refs[k * count : (k + 1) * count]:
            out_ref[at : at + ref.shape[0]] = ref[...]
            at += ref.shape[0]


def emb_kernel(d_own_ref, d_other_ref, c_own_ref, c_other_ref, after_ref, out_ref):
    dims = (((0,), (0,)), ((), ()))
    out_ref[...] = lax.dot_general(
        d_own_ref[...], c_own_ref[...], dims, preferred_element_type=F32
    ) + lax.dot_general(d_other_ref[...], c_other_ref[...], dims, preferred_element_type=F32)


def finish_kernel(grad_ref, received_ref, column_ref, after_hbm, out_ref):
    out_ref[...] = (grad_ref[...] + received_ref[...].astype(F32)) * column_ref[:, :1]


def hbm(count):
    return [pl.BlockSpec(memory_space=pltpu.HBM)] * count


def vmem(count):
    return [pl.BlockSpec(memory_space=pltpu.VMEM)] * count


def keep(*arrays):
    return [pltpu.with_memory_space_constraint(x, pltpu.HBM) for x in arrays]


def cost(flops, nbytes):
    return pl.CostEstimate(flops=flops, bytes_accessed=nbytes, transcendentals=0)


def params(*sizes):
    return pltpu.CompilerParams(vmem_limit_bytes=(2 * sum(sizes) // MIB + 4) * MIB)


def shards(embeddings, classifier, label_valid, shortlist, slot_live, positive, negative):
    lab = lax.axis_size("lab")
    enc = lax.axis_size("enc")
    docs, width = embeddings.shape
    panel = classifier.shape[0]
    slots = shortlist.shape[1]
    half = lab // 2 * panel
    groups = bit_groups(lab)

    negatives = negative.shape[2]
    height = slots * (negatives + 2)
    packed, column, index_own = pl.pallas_call(
        functools.partial(pack_kernel, scale=1.0 / math.sqrt(docs * enc * slots)),
        out_shape=[
            jax.ShapeDtypeStruct((panel, width), BF16),
            jax.ShapeDtypeStruct((panel, LANES), F32),
            jax.ShapeDtypeStruct((height, docs), BF16),
        ],
        in_specs=hbm(6),
        out_specs=vmem(3),
        scratch_shapes=[pltpu.VMEM((panel, width), F32), pltpu.VMEM((1, panel), jnp.int32)]
        + [pltpu.VMEM((slots, docs), jnp.int32)] * 3
        + [pltpu.VMEM((slots, negatives, docs), jnp.int32), pltpu.SemaphoreType.DMA((6,))],
        compiler_params=params(panel * width * 6, height * docs * 4),
        cost_estimate=cost(panel * width, panel * width * 6 + height * docs * 4),
        name="pack",
    )(
        *keep(
            classifier, label_valid.reshape(1, panel), shortlist.T, slot_live.T, positive.T,
            negative.transpose(1, 2, 0),
        )
    )
    pieces = [packed]
    for group in groups:
        own = pieces[0] if len(pieces) == 1 else jnp.concatenate(pieces, 0)
        pieces = [own] + [flip(own, "lab", mask) for mask in group_masks(group)]

    emb_other = flip(embeddings, "lab", 1)
    index_other = flip(index_own, "lab", 1)
    emb_own, own_turned, other_turned = pl.pallas_call(
        turn_kernel,
        out_shape=[jax.ShapeDtypeStruct((docs, width), BF16)]
        + [jax.ShapeDtypeStruct((width, docs), BF16)] * 2,
        in_specs=hbm(1) + vmem(1),
        out_specs=vmem(3),
        scratch_shapes=[pltpu.SemaphoreType.DMA],
        compiler_params=params(docs * width * 10),
        cost_estimate=cost(docs * width, docs * width * 10),
        name="turn",
    )(*keep(embeddings), emb_other)
    target_own, target_other = pl.pallas_call(
        functools.partial(targets_kernel, panel=panel, slots=slots),
        out_shape=[jax.ShapeDtypeStruct((half, docs), BF16)] * 2,
        in_specs=vmem(3),
        out_specs=vmem(2),
        compiler_params=params(height * docs * 8, docs * half * 4),
        cost_estimate=cost(docs * panel * slots * 80, height * docs * 8 + docs * half * 4),
        name="targets",
    )(index_own, index_other, other_turned)

    each = pieces[0].shape[0]
    number = len(pieces)

    def score(which, after):
        count, rows = len(which), each * len(which)
        outs = pl.pallas_call(
            functools.partial(score_kernel, which=which, after=len(after)),
            out_shape=[jax.ShapeDtypeStruct((each, width), BF16 if i else F32) for i in which]
            + [jax.ShapeDtypeStruct((each, docs), BF16)] * (2 * count),
            in_specs=vmem(count + 6 + len(after)),
            out_specs=vmem(3 * count),
            compiler_params=params(8 * docs * width, 16 * rows * docs, 12 * rows * width),
            cost_estimate=cost(
                8 * docs * rows * width, 8 * docs * width + 8 * rows * docs + 8 * rows * width
            ),
            name="score",
        )(
            *[pieces[i] for i in which], emb_own, emb_other, own_turned, other_turned,
            target_own, target_other, *after,
        )
        return outs[:count], outs[count : 2 * count], outs[2 * count :]

    order = [number - 1, 0] + list(range(1, number - 1))
    grads, dlogits = {}, ([], [])
    for which in [w for w in (order[:2], order[2:]) if w]:
        results = score(which, list(grads.values())[:1])
        grads.update(zip(which, results[0]))
        for store, values in zip(dlogits, results[1:]):
            store += values
    classifier_own, d_own, d_theirs = pl.pallas_call(
        functools.partial(join_kernel, count=number),
        out_shape=[jax.ShapeDtypeStruct((half, width), BF16)]
        + [jax.ShapeDtypeStruct((half, docs), BF16)] * 2,
        in_specs=vmem(3 * number),
        out_specs=vmem(3),
        compiler_params=params(4 * half * width, 8 * half * docs),
        cost_estimate=cost(0, 4 * half * width + 8 * half * docs),
        name="join",
    )(*[pieces[i] for i in order], *dlogits[0], *dlogits[1])

    grad = None
    for group in reversed(groups):
        masks = group_masks(group)
        if grad is not None:
            grad = grad.reshape(len(masks) + 1, -1, width)
            grads = [grad[0]] + [grad[i].astype(BF16) for i in range(1, len(masks) + 1)]
        received = []
        for i in reversed(range(len(masks))):
            value = grads[i + 1]
            if i == 2:
                value = jnp.concatenate([value, value[:1]], 0)
            received.append(flip(value, "lab", masks[i])[: grads[i + 1].shape[0]])
        grad = grads[0]
        for r in received:
            grad = grad + r.astype(F32)
    if grad is None:
        grad = grads[0]
    d_other, classifier_other = flip(d_theirs, "lab", 1), flip(classifier_own, "lab", 1)
    bits = [1 << bit for bit in range(enc.bit_length() - 1)]
    for bit in bits[:-1]:
        grad = grad + flip(grad.astype(BF16), "enc", bit).astype(F32)
    received = flip(grad.astype(BF16), "enc", bits[-1])

    emb_grad = pl.pallas_call(
        emb_kernel,
        out_shape=jax.ShapeDtypeStruct((docs, width), F32),
        in_specs=vmem(5),
        out_specs=pl.BlockSpec(memory_space=pltpu.VMEM),
        compiler_params=params(8 * docs * width, 4 * half * docs, 4 * half * width),
        cost_estimate=cost(4 * docs * half * width, 4 * docs * width + 4 * half * docs + 4 * half * width),
        name="emb_grad",
    )(d_own, d_other, classifier_own, classifier_other, grad)

    w_grad = pl.pallas_call(
        finish_kernel,
        out_shape=jax.ShapeDtypeStruct((panel, width), F32),
        in_specs=vmem(3) + hbm(1),
        out_specs=pl.BlockSpec(memory_space=pltpu.VMEM),
        compiler_params=params(panel * width * 10),
        cost_estimate=cost(panel * width, panel * width * 10),
        name="finish",
    )(grad, received, column, *keep(emb_grad))
    return (w_grad, emb_grad)


def solution(mesh):
    in_specs = (
        P(("enc", "lab"), None),
        P("lab", None),
        P("lab"),
        P(("enc", "lab"), None),
        P(("enc", "lab"), None),
        P(("enc", "lab"), None),
        P(("enc", "lab"), None, None),
    )
    out_specs = (P("lab", None), P(("enc", "lab"), None))
    return jax.shard_map(shards, mesh=mesh, in_specs=in_specs, out_specs=out_specs, check_vma=False)
```

```python
import functools
import math

import jax
import jax.numpy as jnp
from jax import lax
from jax.experimental import pallas as pl
from jax.experimental.pallas import tpu as pltpu
from jax.sharding import PartitionSpec as P

BF16 = jnp.bfloat16
F32 = jnp.float32
LANES = 128
PACKED = 16
ROWS = 256
MIB = 1024 * 1024


def flip(value, axis, mask):
    return lax.ppermute(value, axis, [(i, i ^ mask) for i in range(lax.axis_size(axis))])


def bit_groups(count):
    masks = [1 << b for b in range(1, count.bit_length() - 1)]
    return [tuple(masks[i : i + 2]) for i in range(0, len(masks), 2)]


def group_masks(group):
    return [group[0]] if len(group) == 1 else [group[0], group[1], group[0] | group[1]]


def fetch(sources, targets, sem):
    copies = [pltpu.make_async_copy(x, y, sem.at[i]) for i, (x, y) in enumerate(zip(sources, targets))]
    for copy in copies:
        copy.start()
    for copy in copies:
        copy.wait()


def flag_column(flags):
    panel = flags.shape[1]
    diagonal = lax.broadcasted_iota(jnp.int32, (panel, panel), 0) == lax.broadcasted_iota(
        jnp.int32, (panel, panel), 1
    )
    spread = jnp.broadcast_to(flags.astype(F32), (panel, panel))
    return jnp.sum(jnp.where(diagonal, spread, 0.0), axis=1, keepdims=True)


def pack_kernel(
    classifier_hbm, valid_hbm, short_hbm, live_hbm, pos_hbm, neg_hbm, rows_ref, column_ref, index_ref,
    classifier_ref, valid_ref, short_ref, live_ref, pos_ref, neg_ref, sem, *, scale
):
    slots, negatives, docs = neg_ref.shape
    fetch(
        (classifier_hbm, valid_hbm, short_hbm, live_hbm, pos_hbm, neg_hbm),
        (classifier_ref, valid_ref, short_ref, live_ref, pos_ref, neg_ref),
        sem,
    )
    column = flag_column(valid_ref[...])
    rows_ref[...] = (classifier_ref[...] * column).astype(BF16)
    column_ref[...] = jnp.broadcast_to(column * scale, column_ref.shape)
    index_ref[...] = jnp.concatenate(
        [
            neg_ref[...].reshape(slots * negatives, docs),
            pos_ref[...],
            jnp.where(live_ref[...] > 0, short_ref[...], -1),
        ],
        0,
    ).astype(F32).astype(BF16)


def turn_kernel(emb_hbm, other_ref, own_ref, own_turned_ref, other_turned_ref, sem):
    copy = pltpu.make_async_copy(emb_hbm, own_ref, sem)
    copy.start()
    other_turned_ref[...] = other_ref[...].T
    copy.wait()
    own_turned_ref[...] = own_ref[...].T


def targets_kernel(index_own_ref, index_other_ref, after_ref, target_own_ref, target_other_ref, *, panel, slots):
    me = lax.axis_index("lab")
    docs = index_own_ref.shape[1]
    negatives = index_own_ref.shape[0] // slots - 2
    shape = (panel // PACKED, PACKED, LANES)
    label = PACKED * lax.broadcasted_iota(jnp.int32, shape, 0) + lax.broadcasted_iota(jnp.int32, shape, 1)
    label = label.astype(F32).astype(BF16)
    one, zero = jnp.ones((), BF16), jnp.zeros((), BF16)

    def fill(index_ref, out_ref, lanes):
        index = index_ref[:, lanes].astype(F32)

        def row(at):
            return jnp.broadcast_to(index[at : at + 1], (PACKED, LANES))

        values, relative = [], []
        for s in range(slots):
            count = jnp.zeros(shape, BF16)
            for k in range(negatives):
                count = count + jnp.where(row(s * negatives + k).astype(BF16)[None] == label, one, zero)
            hot = row(slots * negatives + s).astype(BF16)[None] == label
            values.append(jnp.where(hot, -one - count, count))
            relative.append(row(slots * (negatives + 1) + s).astype(jnp.int32) ^ me)
        for j in range(out_ref.shape[0] // panel):
            block = jnp.zeros(shape, BF16)
            for s in range(slots):
                chosen = jnp.where(relative[s] == 2 * j, 1.0, 0.0).astype(BF16)
                block = block + chosen[None] * values[s]
            out_ref[pl.ds(j * panel, panel), lanes] = block.reshape(panel, LANES)

    def chunk(i, carry):
        lanes = pl.ds(pl.multiple_of(i * LANES, LANES), LANES)
        fill(index_own_ref, target_own_ref, lanes)
        fill(index_other_ref, target_other_ref, lanes)
        return carry

    lax.fori_loop(0, docs // LANES, chunk, 0)


def score_kernel(*refs, which, after):
    refs = list(refs)

    def take(number):
        return [refs.pop(0) for _ in range(number)]

    count = len(which)
    piece_refs, emb_refs, turned_refs, target_refs = take(count), take(2), take(2), take(2)
    take(after)
    grad_refs, dlogit_refs = take(count), [take(count) for _ in range(2)]
    each = piece_refs[0].shape[0]
    if each * count <= ROWS:
        units = [[(i, 0, each) for i in range(count)]]
    else:
        rows = min(ROWS, each)
        units = [[(i, start, rows)] for i in range(count) for start in range(0, each, rows)]

    def gather(unit, refs, at=lambda i: 0):
        values = [refs[i][at(i) + start : at(i) + start + rows] for i, start, rows in unit]
        return values[0] if len(values) == 1 else jnp.concatenate(values, 0)

    for unit in units:
        block = gather(unit, piece_refs)
        logits = [jnp.dot(block, ref[...], preferred_element_type=F32) for ref in turned_refs]
        dlogits = []
        for x, target_ref in zip(logits, target_refs):
            signed = gather(unit, [target_ref] * count, lambda i: which[i] * each).astype(F32)
            dlogits.append((signed * jax.nn.sigmoid(jnp.where(signed < 0, -x, x))).astype(BF16))
        grad = jnp.dot(
            jnp.concatenate(dlogits, 1),
            jnp.concatenate([ref[...] for ref in emb_refs], 0),
            preferred_element_type=F32,
        )
        off = 0
        for i, start, rows in unit:
            for d, out_refs in zip(dlogits, dlogit_refs):
                out_refs[i][start : start + rows] = d[off : off + rows]
            grad_refs[i][start : start + rows] = grad[off : off + rows].astype(grad_refs[i].dtype)
            off += rows
    for ref in grad_refs:
        if ref.shape[0] > each:
            ref[each:] = jnp.zeros((ref.shape[0] - each, ref.shape[1]), ref.dtype)


def join_kernel(*refs, count):
    for k in range(3):
        out_ref = refs[3 * count + k]
        at = 0
        for ref in refs[k * count : (k + 1) * count]:
            out_ref[at : at + ref.shape[0]] = ref[...]
            at += ref.shape[0]


def emb_kernel(d_own_ref, d_other_ref, c_own_ref, c_other_ref, after_ref, out_ref):
    dims = (((0,), (0,)), ((), ()))
    out_ref[...] = lax.dot_general(
        d_own_ref[...], c_own_ref[...], dims, preferred_element_type=F32
    ) + lax.dot_general(d_other_ref[...], c_other_ref[...], dims, preferred_element_type=F32)


def finish_kernel(grad_ref, received_ref, column_ref, after_hbm, out_ref):
    out_ref[...] = (grad_ref[...] + received_ref[...].astype(F32)) * column_ref[:, :1]


def hbm(count):
    return [pl.BlockSpec(memory_space=pltpu.HBM)] * count


def vmem(count):
    return [pl.BlockSpec(memory_space=pltpu.VMEM)] * count


def keep(*arrays):
    return [pltpu.with_memory_space_constraint(x, pltpu.HBM) for x in arrays]


def cost(flops, nbytes):
    return pl.CostEstimate(flops=flops, bytes_accessed=nbytes, transcendentals=0)


def params(*sizes):
    return pltpu.CompilerParams(vmem_limit_bytes=(2 * sum(sizes) // MIB + 4) * MIB)


def shards(embeddings, classifier, label_valid, shortlist, slot_live, positive, negative):
    lab = lax.axis_size("lab")
    enc = lax.axis_size("enc")
    docs, width = embeddings.shape
    panel = classifier.shape[0]
    slots = shortlist.shape[1]
    half = lab // 2 * panel
    groups = bit_groups(lab)

    negatives = negative.shape[2]
    height = slots * (negatives + 2)
    packed, column, index_own = pl.pallas_call(
        functools.partial(pack_kernel, scale=1.0 / math.sqrt(docs * enc * slots)),
        out_shape=[
            jax.ShapeDtypeStruct((panel, width), BF16),
            jax.ShapeDtypeStruct((panel, LANES), F32),
            jax.ShapeDtypeStruct((height, docs), BF16),
        ],
        in_specs=hbm(6),
        out_specs=vmem(3),
        scratch_shapes=[pltpu.VMEM((panel, width), F32), pltpu.VMEM((1, panel), jnp.int32)]
        + [pltpu.VMEM((slots, docs), jnp.int32)] * 3
        + [pltpu.VMEM((slots, negatives, docs), jnp.int32), pltpu.SemaphoreType.DMA((6,))],
        compiler_params=params(panel * width * 6, height * docs * 4),
        cost_estimate=cost(panel * width, panel * width * 6 + height * docs * 4),
        name="pack",
    )(
        *keep(
            classifier, label_valid.reshape(1, panel), shortlist.T, slot_live.T, positive.T,
            negative.transpose(1, 2, 0),
        )
    )
    pieces = [packed]
    for group in groups:
        own = pieces[0] if len(pieces) == 1 else jnp.concatenate(pieces, 0)
        pieces = [own] + [flip(own, "lab", mask) for mask in group_masks(group)]

    emb_other = flip(embeddings, "lab", 1)
    index_other = flip(index_own, "lab", 1)
    emb_own, own_turned, other_turned = pl.pallas_call(
        turn_kernel,
        out_shape=[jax.ShapeDtypeStruct((docs, width), BF16)]
        + [jax.ShapeDtypeStruct((width, docs), BF16)] * 2,
        in_specs=hbm(1) + vmem(1),
        out_specs=vmem(3),
        scratch_shapes=[pltpu.SemaphoreType.DMA],
        compiler_params=params(docs * width * 10),
        cost_estimate=cost(docs * width, docs * width * 10),
        name="turn",
    )(*keep(embeddings), emb_other)
    target_own, target_other = pl.pallas_call(
        functools.partial(targets_kernel, panel=panel, slots=slots),
        out_shape=[jax.ShapeDtypeStruct((half, docs), BF16)] * 2,
        in_specs=vmem(3),
        out_specs=vmem(2),
        compiler_params=params(height * docs * 8, docs * half * 4),
        cost_estimate=cost(docs * panel * slots * 80, height * docs * 8 + docs * half * 4),
        name="targets",
    )(index_own, index_other, other_turned)

    each = pieces[0].shape[0]
    number = len(pieces)

    def score(which, after):
        count, rows = len(which), each * len(which)
        outs = pl.pallas_call(
            functools.partial(score_kernel, which=which, after=len(after)),
            out_shape=[
                jax.ShapeDtypeStruct((each + (PACKED if i == 3 else 0), width), BF16 if i else F32)
                for i in which
            ]
            + [jax.ShapeDtypeStruct((each, docs), BF16)] * (2 * count),
            in_specs=vmem(count + 6 + len(after)),
            out_specs=vmem(3 * count),
            compiler_params=params(8 * docs * width, 16 * rows * docs, 12 * rows * width),
            cost_estimate=cost(
                8 * docs * rows * width, 8 * docs * width + 8 * rows * docs + 8 * rows * width
            ),
            name="score",
        )(
            *[pieces[i] for i in which], emb_own, emb_other, own_turned, other_turned,
            target_own, target_other, *after,
        )
        return outs[:count], outs[count : 2 * count], outs[2 * count :]

    order = [number - 1, 0] + list(range(1, number - 1))
    grads, dlogits = {}, ([], [])
    for which in [w for w in (order[:2], order[2:]) if w]:
        results = score(which, list(grads.values())[:1])
        grads.update(zip(which, results[0]))
        for store, values in zip(dlogits, results[1:]):
            store += values
    classifier_own, d_own, d_theirs = pl.pallas_call(
        functools.partial(join_kernel, count=number),
        out_shape=[jax.ShapeDtypeStruct((half, width), BF16)]
        + [jax.ShapeDtypeStruct((half, docs), BF16)] * 2,
        in_specs=vmem(3 * number),
        out_specs=vmem(3),
        compiler_params=params(4 * half * width, 8 * half * docs),
        cost_estimate=cost(0, 4 * half * width + 8 * half * docs),
        name="join",
    )(*[pieces[i] for i in order], *dlogits[0], *dlogits[1])

    grad = None
    for group in reversed(groups):
        masks = group_masks(group)
        if grad is not None:
            grad = grad.reshape(len(masks) + 1, -1, width)
            grads = [grad[0]] + [grad[i].astype(BF16) for i in range(1, len(masks) + 1)]
        received = []
        for i in reversed(range(len(masks))):
            value = grads[i + 1]
            if i == 2 and value.shape[0] == grads[0].shape[0]:
                value = jnp.concatenate([value, value[:1]], 0)
            received.append(flip(value, "lab", masks[i])[: grads[0].shape[0]])
        grad = grads[0]
        for r in received:
            grad = grad + r.astype(F32)
    if grad is None:
        grad = grads[0]
    d_other, classifier_other = flip(d_theirs, "lab", 1), flip(classifier_own, "lab", 1)
    bits = [1 << bit for bit in range(enc.bit_length() - 1)]

    def along(value, even, odd):
        pairs = [(i, i ^ lab * (odd if i & 1 else even)) for i in range(enc * lab)]
        return lax.ppermute(value, ("enc", "lab"), pairs)

    for even, odd in list(zip(bits, reversed(bits)))[:-1]:
        grad = grad + along(grad.astype(BF16), even, odd).astype(F32)
    received = along(grad.astype(BF16), bits[-1], bits[0])

    emb_grad = pl.pallas_call(
        emb_kernel,
        out_shape=jax.ShapeDtypeStruct((docs, width), F32),
        in_specs=vmem(5),
        out_specs=pl.BlockSpec(memory_space=pltpu.VMEM),
        compiler_params=params(8 * docs * width, 4 * half * docs, 4 * half * width),
        cost_estimate=cost(4 * docs * half * width, 4 * docs * width + 4 * half * docs + 4 * half * width),
        name="emb_grad",
    )(d_own, d_other, classifier_own, classifier_other, grad)

    w_grad = pl.pallas_call(
        finish_kernel,
        out_shape=jax.ShapeDtypeStruct((panel, width), F32),
        in_specs=vmem(3) + hbm(1),
        out_specs=pl.BlockSpec(memory_space=pltpu.VMEM),
        compiler_params=params(panel * width * 10),
        cost_estimate=cost(panel * width, panel * width * 10),
        name="finish",
    )(grad, received, column, *keep(emb_grad))
    return (w_grad, emb_grad)


def solution(mesh):
    in_specs = (
        P(("enc", "lab"), None),
        P("lab", None),
        P("lab"),
        P(("enc", "lab"), None),
        P(("enc", "lab"), None),
        P(("enc", "lab"), None),
        P(("enc", "lab"), None, None),
    )
    out_specs = (P("lab", None), P(("enc", "lab"), None))
    return jax.shard_map(shards, mesh=mesh, in_specs=in_specs, out_specs=out_specs, check_vma=False)
```

```python
import functools
import math

import jax
import jax.numpy as jnp
from jax import lax
from jax.experimental import pallas as pl
from jax.experimental.pallas import tpu as pltpu
from jax.sharding import PartitionSpec as P

BF16 = jnp.bfloat16
F32 = jnp.float32
LANES = 128
PACKED = 16
ROWS = 256
MIB = 1024 * 1024


def flip(value, axis, mask):
    return lax.ppermute(value, axis, [(i, i ^ mask) for i in range(lax.axis_size(axis))])


def bit_groups(count):
    masks = [1 << b for b in range(1, count.bit_length() - 1)]
    return [tuple(masks[i : i + 2]) for i in range(0, len(masks), 2)]


def group_masks(group):
    return [group[0]] if len(group) == 1 else [group[0], group[1], group[0] | group[1]]


def fetch(sources, targets, sem):
    copies = [pltpu.make_async_copy(x, y, sem.at[i]) for i, (x, y) in enumerate(zip(sources, targets))]
    for copy in copies:
        copy.start()
    for copy in copies:
        copy.wait()


def flag_column(flags):
    panel = flags.shape[1]
    diagonal = lax.broadcasted_iota(jnp.int32, (panel, panel), 0) == lax.broadcasted_iota(
        jnp.int32, (panel, panel), 1
    )
    spread = jnp.broadcast_to(flags.astype(F32), (panel, panel))
    return jnp.sum(jnp.where(diagonal, spread, 0.0), axis=1, keepdims=True)


def pack_kernel(
    classifier_hbm, valid_hbm, short_hbm, live_hbm, pos_hbm, neg_hbm, rows_ref, column_ref, index_ref,
    classifier_ref, valid_ref, short_ref, live_ref, pos_ref, neg_ref, sem, *, scale
):
    slots, negatives, docs = neg_ref.shape
    fetch(
        (classifier_hbm, valid_hbm, short_hbm, live_hbm, pos_hbm, neg_hbm),
        (classifier_ref, valid_ref, short_ref, live_ref, pos_ref, neg_ref),
        sem,
    )
    column = flag_column(valid_ref[...])
    rows_ref[...] = (classifier_ref[...] * column).astype(BF16)
    column_ref[...] = jnp.broadcast_to(column * scale, column_ref.shape)
    index_ref[...] = jnp.concatenate(
        [
            neg_ref[...].reshape(slots * negatives, docs),
            pos_ref[...],
            jnp.where(live_ref[...] > 0, short_ref[...], -1),
        ],
        0,
    ).astype(F32).astype(BF16)


def turn_kernel(emb_hbm, other_ref, own_ref, own_turned_ref, other_turned_ref, sem):
    copy = pltpu.make_async_copy(emb_hbm, own_ref, sem)
    copy.start()
    other_turned_ref[...] = other_ref[...].T
    copy.wait()
    own_turned_ref[...] = own_ref[...].T


def targets_kernel(index_own_ref, index_other_ref, after_ref, target_own_ref, target_other_ref, *, panel, slots):
    me = lax.axis_index("lab")
    docs = index_own_ref.shape[1]
    negatives = index_own_ref.shape[0] // slots - 2
    shape = (panel // PACKED, PACKED, LANES)
    label = PACKED * lax.broadcasted_iota(jnp.int32, shape, 0) + lax.broadcasted_iota(jnp.int32, shape, 1)
    label = label.astype(F32).astype(BF16)
    one, zero = jnp.ones((), BF16), jnp.zeros((), BF16)

    def fill(index_ref, out_ref, lanes):
        index = index_ref[:, lanes].astype(F32)

        def row(at):
            return jnp.broadcast_to(index[at : at + 1], (PACKED, LANES))

        values, relative = [], []
        for s in range(slots):
            count = jnp.zeros(shape, BF16)
            for k in range(negatives):
                count = count + jnp.where(row(s * negatives + k).astype(BF16)[None] == label, one, zero)
            hot = row(slots * negatives + s).astype(BF16)[None] == label
            values.append(jnp.where(hot, -one - count, count))
            relative.append(row(slots * (negatives + 1) + s).astype(jnp.int32) ^ me)
        for j in range(out_ref.shape[0] // panel):
            block = jnp.zeros(shape, BF16)
            for s in range(slots):
                chosen = jnp.where(relative[s] == 2 * j, 1.0, 0.0).astype(BF16)
                block = block + chosen[None] * values[s]
            out_ref[pl.ds(j * panel, panel), lanes] = block.reshape(panel, LANES)

    def chunk(i, carry):
        lanes = pl.ds(pl.multiple_of(i * LANES, LANES), LANES)
        fill(index_own_ref, target_own_ref, lanes)
        fill(index_other_ref, target_other_ref, lanes)
        return carry

    lax.fori_loop(0, docs // LANES, chunk, 0)


def score_kernel(*refs, which, after):
    refs = list(refs)

    def take(number):
        return [refs.pop(0) for _ in range(number)]

    count = len(which)
    piece_refs, emb_refs, turned_refs, target_refs = take(count), take(2), take(2), take(2)
    take(after)
    grad_refs, dlogit_refs = take(count), [take(count) for _ in range(2)]
    each = piece_refs[0].shape[0]
    if each * count <= ROWS:
        units = [[(i, 0, each) for i in range(count)]]
    else:
        rows = min(ROWS, each)
        units = [[(i, start, rows)] for i in range(count) for start in range(0, each, rows)]

    def gather(unit, refs, at=lambda i: 0):
        values = [refs[i][at(i) + start : at(i) + start + rows] for i, start, rows in unit]
        return values[0] if len(values) == 1 else jnp.concatenate(values, 0)

    for unit in units:
        block = gather(unit, piece_refs)
        logits = [jnp.dot(block, ref[...], preferred_element_type=F32) for ref in turned_refs]
        dlogits = []
        for x, target_ref in zip(logits, target_refs):
            signed = gather(unit, [target_ref] * count, lambda i: which[i] * each).astype(F32)
            dlogits.append((signed * jax.nn.sigmoid(jnp.where(signed < 0, -x, x))).astype(BF16))
        grad = jnp.dot(
            jnp.concatenate(dlogits, 1),
            jnp.concatenate([ref[...] for ref in emb_refs], 0),
            preferred_element_type=F32,
        )
        off = 0
        for i, start, rows in unit:
            for d, out_refs in zip(dlogits, dlogit_refs):
                out_refs[i][start : start + rows] = d[off : off + rows]
            grad_refs[i][start : start + rows] = grad[off : off + rows].astype(grad_refs[i].dtype)
            off += rows


def join_kernel(*refs, count):
    for k in range(3):
        out_ref = refs[3 * count + k]
        at = 0
        for ref in refs[k * count : (k + 1) * count]:
            out_ref[at : at + ref.shape[0]] = ref[...]
            at += ref.shape[0]


def emb_kernel(d_own_ref, d_other_ref, c_own_ref, c_other_ref, after_ref, out_ref):
    dims = (((0,), (0,)), ((), ()))
    out_ref[...] = lax.dot_general(
        d_own_ref[...], c_own_ref[...], dims, preferred_element_type=F32
    ) + lax.dot_general(d_other_ref[...], c_other_ref[...], dims, preferred_element_type=F32)


def finish_kernel(grad_ref, received_ref, column_ref, after_hbm, out_ref):
    out_ref[...] = (grad_ref[...] + received_ref[...].astype(F32)) * column_ref[:, :1]


def hbm(count):
    return [pl.BlockSpec(memory_space=pltpu.HBM)] * count


def vmem(count):
    return [pl.BlockSpec(memory_space=pltpu.VMEM)] * count


def keep(*arrays):
    return [pltpu.with_memory_space_constraint(x, pltpu.HBM) for x in arrays]


def cost(flops, nbytes):
    return pl.CostEstimate(flops=flops, bytes_accessed=nbytes, transcendentals=0)


def params(*sizes):
    return pltpu.CompilerParams(vmem_limit_bytes=(2 * sum(sizes) // MIB + 4) * MIB)


def shards(embeddings, classifier, label_valid, shortlist, slot_live, positive, negative):
    lab = lax.axis_size("lab")
    enc = lax.axis_size("enc")
    docs, width = embeddings.shape
    panel = classifier.shape[0]
    slots = shortlist.shape[1]
    half = lab // 2 * panel
    groups = bit_groups(lab)

    negatives = negative.shape[2]
    height = slots * (negatives + 2)
    packed, column, index_own = pl.pallas_call(
        functools.partial(pack_kernel, scale=1.0 / math.sqrt(docs * enc * slots)),
        out_shape=[
            jax.ShapeDtypeStruct((panel, width), BF16),
            jax.ShapeDtypeStruct((panel, LANES), F32),
            jax.ShapeDtypeStruct((height, docs), BF16),
        ],
        in_specs=hbm(6),
        out_specs=vmem(3),
        scratch_shapes=[pltpu.VMEM((panel, width), F32), pltpu.VMEM((1, panel), jnp.int32)]
        + [pltpu.VMEM((slots, docs), jnp.int32)] * 3
        + [pltpu.VMEM((slots, negatives, docs), jnp.int32), pltpu.SemaphoreType.DMA((6,))],
        compiler_params=params(panel * width * 6, height * docs * 4),
        cost_estimate=cost(panel * width, panel * width * 6 + height * docs * 4),
        name="pack",
    )(
        *keep(
            classifier, label_valid.reshape(1, panel), shortlist.T, slot_live.T, positive.T,
            negative.transpose(1, 2, 0),
        )
    )
    pieces = [packed]
    for group in groups:
        own = pieces[0] if len(pieces) == 1 else jnp.concatenate(pieces, 0)
        pieces = [own] + [flip(own, "lab", mask) for mask in group_masks(group)]

    emb_other = flip(embeddings, "lab", 1)
    index_other = flip(index_own, "lab", 1)
    emb_own, own_turned, other_turned = pl.pallas_call(
        turn_kernel,
        out_shape=[jax.ShapeDtypeStruct((docs, width), BF16)]
        + [jax.ShapeDtypeStruct((width, docs), BF16)] * 2,
        in_specs=hbm(1) + vmem(1),
        out_specs=vmem(3),
        scratch_shapes=[pltpu.SemaphoreType.DMA],
        compiler_params=params(docs * width * 10),
        cost_estimate=cost(docs * width, docs * width * 10),
        name="turn",
    )(*keep(embeddings), emb_other)
    target_own, target_other = pl.pallas_call(
        functools.partial(targets_kernel, panel=panel, slots=slots),
        out_shape=[jax.ShapeDtypeStruct((half, docs), BF16)] * 2,
        in_specs=vmem(3),
        out_specs=vmem(2),
        compiler_params=params(height * docs * 8, docs * half * 4),
        cost_estimate=cost(docs * panel * slots * 80, height * docs * 8 + docs * half * 4),
        name="targets",
    )(index_own, index_other, other_turned)

    each = pieces[0].shape[0]
    number = len(pieces)

    def score(which, after):
        count, rows = len(which), each * len(which)
        outs = pl.pallas_call(
            functools.partial(score_kernel, which=which, after=len(after)),
            out_shape=[jax.ShapeDtypeStruct((each, width), BF16 if i else F32) for i in which]
            + [jax.ShapeDtypeStruct((each, docs), BF16)] * (2 * count),
            in_specs=vmem(count + 6 + len(after)),
            out_specs=vmem(3 * count),
            compiler_params=params(8 * docs * width, 16 * rows * docs, 12 * rows * width),
            cost_estimate=cost(
                8 * docs * rows * width, 8 * docs * width + 8 * rows * docs + 8 * rows * width
            ),
            name="score",
        )(
            *[pieces[i] for i in which], emb_own, emb_other, own_turned, other_turned,
            target_own, target_other, *after,
        )
        return outs[:count], outs[count : 2 * count], outs[2 * count :]

    order = [number - 1, 0] + list(range(1, number - 1))
    grads, dlogits = {}, ([], [])
    for which in [w for w in (order[:2], order[2:]) if w]:
        results = score(which, list(grads.values())[:1])
        grads.update(zip(which, results[0]))
        for store, values in zip(dlogits, results[1:]):
            store += values
    classifier_own, d_own, d_theirs = pl.pallas_call(
        functools.partial(join_kernel, count=number),
        out_shape=[jax.ShapeDtypeStruct((half, width), BF16)]
        + [jax.ShapeDtypeStruct((half, docs), BF16)] * 2,
        in_specs=vmem(3 * number),
        out_specs=vmem(3),
        compiler_params=params(4 * half * width, 8 * half * docs),
        cost_estimate=cost(0, 4 * half * width + 8 * half * docs),
        name="join",
    )(*[pieces[i] for i in order], *dlogits[0], *dlogits[1])

    grad = None
    for group in reversed(groups):
        masks = group_masks(group)
        if grad is not None:
            grad = grad.reshape(len(masks) + 1, -1, width)
            grads = [grad[0]] + [grad[i].astype(BF16) for i in range(1, len(masks) + 1)]
        received = []
        for i in reversed(range(len(masks))):
            value = grads[i + 1]
            if i == 2:
                value = jnp.concatenate([value, value[:1]], 0)
            received.append(flip(value, "lab", masks[i])[: grads[i + 1].shape[0]])
        grad = grads[0]
        for r in received:
            grad = grad + r.astype(F32)
    if grad is None:
        grad = grads[0]
    d_other, classifier_other = flip(d_theirs, "lab", 1), flip(classifier_own, "lab", 1)
    bits = [1 << bit for bit in range(enc.bit_length() - 1)]

    def along(value, even, odd):
        pairs = [(i, i ^ lab * (odd if i & 1 else even)) for i in range(enc * lab)]
        return lax.ppermute(value, ("enc", "lab"), pairs)

    for even, odd in list(zip(bits, reversed(bits)))[:-1]:
        grad = grad + along(grad.astype(BF16), even, odd).astype(F32)
    received = along(grad.astype(BF16), bits[-1], bits[0])

    emb_grad = pl.pallas_call(
        emb_kernel,
        out_shape=jax.ShapeDtypeStruct((docs, width), F32),
        in_specs=vmem(5),
        out_specs=pl.BlockSpec(memory_space=pltpu.VMEM),
        compiler_params=params(8 * docs * width, 4 * half * docs, 4 * half * width),
        cost_estimate=cost(4 * docs * half * width, 4 * docs * width + 4 * half * docs + 4 * half * width),
        name="emb_grad",
    )(d_own, d_other, classifier_own, classifier_other, grad)

    w_grad = pl.pallas_call(
        finish_kernel,
        out_shape=jax.ShapeDtypeStruct((panel, width), F32),
        in_specs=vmem(3) + hbm(1),
        out_specs=pl.BlockSpec(memory_space=pltpu.VMEM),
        compiler_params=params(panel * width * 10),
        cost_estimate=cost(panel * width, panel * width * 10),
        name="finish",
    )(grad, received, column, *keep(emb_grad))
    return (w_grad, emb_grad)


def solution(mesh):
    in_specs = (
        P(("enc", "lab"), None),
        P("lab", None),
        P("lab"),
        P(("enc", "lab"), None),
        P(("enc", "lab"), None),
        P(("enc", "lab"), None),
        P(("enc", "lab"), None, None),
    )
    out_specs = (P("lab", None), P(("enc", "lab"), None))
    return jax.shard_map(shards, mesh=mesh, in_specs=in_specs, out_specs=out_specs, check_vma=False)
```

```python
import functools
import math

import jax
import jax.numpy as jnp
from jax import lax
from jax.experimental import pallas as pl
from jax.experimental.pallas import tpu as pltpu
from jax.sharding import PartitionSpec as P

BF16 = jnp.bfloat16
F32 = jnp.float32
LANES = 128
PACKED = 16
ROWS = 256
MIB = 1024 * 1024


def flip(value, axis, mask):
    return lax.ppermute(value, axis, [(i, i ^ mask) for i in range(lax.axis_size(axis))])


def bit_groups(count):
    masks = [1 << b for b in range(1, count.bit_length() - 1)]
    return [tuple(masks[i : i + 2]) for i in range(0, len(masks), 2)]


def group_masks(group):
    return [group[0]] if len(group) == 1 else [group[0], group[1], group[0] | group[1]]


def fetch(sources, targets, sem):
    copies = [pltpu.make_async_copy(x, y, sem.at[i]) for i, (x, y) in enumerate(zip(sources, targets))]
    for copy in copies:
        copy.start()
    for copy in copies:
        copy.wait()


def flag_column(flags):
    panel = flags.shape[1]
    diagonal = lax.broadcasted_iota(jnp.int32, (panel, panel), 0) == lax.broadcasted_iota(
        jnp.int32, (panel, panel), 1
    )
    spread = jnp.broadcast_to(flags.astype(F32), (panel, panel))
    return jnp.sum(jnp.where(diagonal, spread, 0.0), axis=1, keepdims=True)


def pack_kernel(
    classifier_hbm, valid_hbm, short_hbm, live_hbm, pos_hbm, neg_hbm, rows_ref, column_ref, index_ref,
    classifier_ref, valid_ref, short_ref, live_ref, pos_ref, neg_ref, sem, *, scale
):
    slots, negatives, docs = neg_ref.shape
    fetch(
        (classifier_hbm, valid_hbm, short_hbm, live_hbm, pos_hbm, neg_hbm),
        (classifier_ref, valid_ref, short_ref, live_ref, pos_ref, neg_ref),
        sem,
    )
    column = flag_column(valid_ref[...])
    rows_ref[...] = (classifier_ref[...] * column).astype(BF16)
    column_ref[...] = jnp.broadcast_to(column * scale, column_ref.shape)
    index_ref[...] = jnp.concatenate(
        [
            neg_ref[...].reshape(slots * negatives, docs),
            pos_ref[...],
            jnp.where(live_ref[...] > 0, short_ref[...], -1),
        ],
        0,
    ).astype(F32).astype(BF16)


def turn_kernel(emb_hbm, other_ref, own_ref, own_turned_ref, other_turned_ref, sem):
    copy = pltpu.make_async_copy(emb_hbm, own_ref, sem)
    copy.start()
    other_turned_ref[...] = other_ref[...].T
    copy.wait()
    own_turned_ref[...] = own_ref[...].T


def targets_kernel(index_own_ref, index_other_ref, after_ref, target_own_ref, target_other_ref, *, panel, slots):
    me = lax.axis_index("lab")
    docs = index_own_ref.shape[1]
    negatives = index_own_ref.shape[0] // slots - 2
    shape = (panel // PACKED, PACKED, LANES)
    label = PACKED * lax.broadcasted_iota(jnp.int32, shape, 0) + lax.broadcasted_iota(jnp.int32, shape, 1)
    label = label.astype(F32).astype(BF16)
    one, zero = jnp.ones((), BF16), jnp.zeros((), BF16)

    def fill(index_ref, out_ref, lanes):
        index = index_ref[:, lanes].astype(F32)

        def row(at):
            return jnp.broadcast_to(index[at : at + 1], (PACKED, LANES))

        values, relative = [], []
        for s in range(slots):
            count = jnp.zeros(shape, BF16)
            for k in range(negatives):
                count = count + jnp.where(row(s * negatives + k).astype(BF16)[None] == label, one, zero)
            hot = row(slots * negatives + s).astype(BF16)[None] == label
            values.append(jnp.where(hot, -one - count, count))
            relative.append(row(slots * (negatives + 1) + s).astype(jnp.int32) ^ me)
        for j in range(out_ref.shape[0] // panel):
            block = jnp.zeros(shape, BF16)
            for s in range(slots):
                chosen = jnp.where(relative[s] == 2 * j, 1.0, 0.0).astype(BF16)
                block = block + chosen[None] * values[s]
            out_ref[pl.ds(j * panel, panel), lanes] = block.reshape(panel, LANES)

    def chunk(i, carry):
        lanes = pl.ds(pl.multiple_of(i * LANES, LANES), LANES)
        fill(index_own_ref, target_own_ref, lanes)
        fill(index_other_ref, target_other_ref, lanes)
        return carry

    lax.fori_loop(0, docs // LANES, chunk, 0)


def score_kernel(*refs, which, after):
    refs = list(refs)

    def take(number):
        return [refs.pop(0) for _ in range(number)]

    count = len(which)
    piece_refs, emb_refs, turned_refs, target_refs = take(count), take(2), take(2), take(2)
    take(after)
    grad_refs, dlogit_refs = take(count), [take(count) for _ in range(2)]
    each = piece_refs[0].shape[0]
    if each * count <= ROWS:
        units = [[(i, 0, each) for i in range(count)]]
    else:
        rows = min(ROWS, each)
        units = [[(i, start, rows)] for i in range(count) for start in range(0, each, rows)]

    def gather(unit, refs, at=lambda i: 0):
        values = [refs[i][at(i) + start : at(i) + start + rows] for i, start, rows in unit]
        return values[0] if len(values) == 1 else jnp.concatenate(values, 0)

    for unit in units:
        block = gather(unit, piece_refs)
        logits = [jnp.dot(block, ref[...], preferred_element_type=F32) for ref in turned_refs]
        dlogits = []
        for x, target_ref in zip(logits, target_refs):
            signed = gather(unit, [target_ref] * count, lambda i: which[i] * each).astype(F32)
            dlogits.append((signed * jax.nn.sigmoid(jnp.where(signed < 0, -x, x))).astype(BF16))
        grad = jnp.dot(
            jnp.concatenate(dlogits, 1),
            jnp.concatenate([ref[...] for ref in emb_refs], 0),
            preferred_element_type=F32,
        )
        off = 0
        for i, start, rows in unit:
            for d, out_refs in zip(dlogits, dlogit_refs):
                out_refs[i][start : start + rows] = d[off : off + rows]
            grad_refs[i][start : start + rows] = grad[off : off + rows].astype(grad_refs[i].dtype)
            off += rows
    for ref in grad_refs:
        if ref.shape[0] > each:
            ref[each:] = jnp.zeros((ref.shape[0] - each, ref.shape[1]), ref.dtype)


def join_kernel(*refs, count):
    for k in range(3):
        out_ref = refs[3 * count + k]
        at = 0
        for ref in refs[k * count : (k + 1) * count]:
            out_ref[at : at + ref.shape[0]] = ref[...]
            at += ref.shape[0]


def emb_kernel(d_own_ref, d_other_ref, c_own_ref, c_other_ref, after_ref, out_ref):
    dims = (((0,), (0,)), ((), ()))
    out_ref[...] = lax.dot_general(
        d_own_ref[...], c_own_ref[...], dims, preferred_element_type=F32
    ) + lax.dot_general(d_other_ref[...], c_other_ref[...], dims, preferred_element_type=F32)


def finish_kernel(grad_ref, received_ref, column_ref, after_hbm, out_ref):
    out_ref[...] = (grad_ref[...] + received_ref[...].astype(F32)) * column_ref[:, :1]


def hbm(count):
    return [pl.BlockSpec(memory_space=pltpu.HBM)] * count


def vmem(count):
    return [pl.BlockSpec(memory_space=pltpu.VMEM)] * count


def keep(*arrays):
    return [pltpu.with_memory_space_constraint(x, pltpu.HBM) for x in arrays]


def cost(flops, nbytes):
    return pl.CostEstimate(flops=flops, bytes_accessed=nbytes, transcendentals=0)


def params(*sizes):
    return pltpu.CompilerParams(vmem_limit_bytes=(2 * sum(sizes) // MIB + 4) * MIB)


def shards(embeddings, classifier, label_valid, shortlist, slot_live, positive, negative):
    lab = lax.axis_size("lab")
    enc = lax.axis_size("enc")
    docs, width = embeddings.shape
    panel = classifier.shape[0]
    slots = shortlist.shape[1]
    half = lab // 2 * panel
    groups = bit_groups(lab)

    negatives = negative.shape[2]
    height = slots * (negatives + 2)
    packed, column, index_own = pl.pallas_call(
        functools.partial(pack_kernel, scale=1.0 / math.sqrt(docs * enc * slots)),
        out_shape=[
            jax.ShapeDtypeStruct((panel, width), BF16),
            jax.ShapeDtypeStruct((panel, LANES), F32),
            jax.ShapeDtypeStruct((height, docs), BF16),
        ],
        in_specs=hbm(6),
        out_specs=vmem(3),
        scratch_shapes=[pltpu.VMEM((panel, width), F32), pltpu.VMEM((1, panel), jnp.int32)]
        + [pltpu.VMEM((slots, docs), jnp.int32)] * 3
        + [pltpu.VMEM((slots, negatives, docs), jnp.int32), pltpu.SemaphoreType.DMA((6,))],
        compiler_params=params(panel * width * 6, height * docs * 4),
        cost_estimate=cost(panel * width, panel * width * 6 + height * docs * 4),
        name="pack",
    )(
        *keep(
            classifier, label_valid.reshape(1, panel), shortlist.T, slot_live.T, positive.T,
            negative.transpose(1, 2, 0),
        )
    )
    pieces = [packed]
    for group in groups:
        own = pieces[0] if len(pieces) == 1 else jnp.concatenate(pieces, 0)
        pieces = [own] + [flip(own, "lab", mask) for mask in group_masks(group)]

    emb_other = flip(embeddings, "lab", 1)
    index_other = flip(index_own, "lab", 1)
    emb_own, own_turned, other_turned = pl.pallas_call(
        turn_kernel,
        out_shape=[jax.ShapeDtypeStruct((docs, width), BF16)]
        + [jax.ShapeDtypeStruct((width, docs), BF16)] * 2,
        in_specs=hbm(1) + vmem(1),
        out_specs=vmem(3),
        scratch_shapes=[pltpu.SemaphoreType.DMA],
        compiler_params=params(docs * width * 10),
        cost_estimate=cost(docs * width, docs * width * 10),
        name="turn",
    )(*keep(embeddings), emb_other)
    target_own, target_other = pl.pallas_call(
        functools.partial(targets_kernel, panel=panel, slots=slots),
        out_shape=[jax.ShapeDtypeStruct((half, docs), BF16)] * 2,
        in_specs=vmem(3),
        out_specs=vmem(2),
        compiler_params=params(height * docs * 8, docs * half * 4),
        cost_estimate=cost(docs * panel * slots * 80, height * docs * 8 + docs * half * 4),
        name="targets",
    )(index_own, index_other, other_turned)

    each = pieces[0].shape[0]
    number = len(pieces)

    def score(which, after):
        count, rows = len(which), each * len(which)
        outs = pl.pallas_call(
            functools.partial(score_kernel, which=which, after=len(after)),
            out_shape=[
                jax.ShapeDtypeStruct((each + (PACKED if i == 3 else 0), width), BF16 if i else F32)
                for i in which
            ]
            + [jax.ShapeDtypeStruct((each, docs), BF16)] * (2 * count),
            in_specs=vmem(count + 6 + len(after)),
            out_specs=vmem(3 * count),
            compiler_params=params(8 * docs * width, 16 * rows * docs, 12 * rows * width),
            cost_estimate=cost(
                8 * docs * rows * width, 8 * docs * width + 8 * rows * docs + 8 * rows * width
            ),
            name="score",
        )(
            *[pieces[i] for i in which], emb_own, emb_other, own_turned, other_turned,
            target_own, target_other, *after,
        )
        return outs[:count], outs[count : 2 * count], outs[2 * count :]

    order = [number - 1, 0] + list(range(1, number - 1))
    grads, dlogits = {}, ([], [])
    for which in [w for w in (order[:2], order[2:]) if w]:
        results = score(which, list(grads.values())[:1])
        grads.update(zip(which, results[0]))
        for store, values in zip(dlogits, results[1:]):
            store += values
    classifier_own, d_own, d_theirs = pl.pallas_call(
        functools.partial(join_kernel, count=number),
        out_shape=[jax.ShapeDtypeStruct((half, width), BF16)]
        + [jax.ShapeDtypeStruct((half, docs), BF16)] * 2,
        in_specs=vmem(3 * number),
        out_specs=vmem(3),
        compiler_params=params(4 * half * width, 8 * half * docs),
        cost_estimate=cost(0, 4 * half * width + 8 * half * docs),
        name="join",
    )(*[pieces[i] for i in order], *dlogits[0], *dlogits[1])

    grad = None
    for group in reversed(groups):
        masks = group_masks(group)
        if grad is not None:
            grad = grad.reshape(len(masks) + 1, -1, width)
            grads = [grad[0]] + [grad[i].astype(BF16) for i in range(1, len(masks) + 1)]
        received = []
        for i in reversed(range(len(masks))):
            value = grads[i + 1]
            if i == 2 and value.shape[0] == grads[0].shape[0]:
                value = jnp.concatenate([value, value[:1]], 0)
            received.append(flip(value, "lab", masks[i])[: grads[0].shape[0]])
        grad = grads[0]
        for r in received:
            grad = grad + r.astype(F32)
    if grad is None:
        grad = grads[0]
    d_other, classifier_other = flip(d_theirs, "lab", 1), flip(classifier_own, "lab", 1)
    bits = [1 << bit for bit in range(enc.bit_length() - 1)]
    for bit in bits[:-1]:
        grad = grad + flip(grad.astype(BF16), "enc", bit).astype(F32)
    received = flip(grad.astype(BF16), "enc", bits[-1])

    emb_grad = pl.pallas_call(
        emb_kernel,
        out_shape=jax.ShapeDtypeStruct((docs, width), F32),
        in_specs=vmem(5),
        out_specs=pl.BlockSpec(memory_space=pltpu.VMEM),
        compiler_params=params(8 * docs * width, 4 * half * docs, 4 * half * width),
        cost_estimate=cost(4 * docs * half * width, 4 * docs * width + 4 * half * docs + 4 * half * width),
        name="emb_grad",
    )(d_own, d_other, classifier_own, classifier_other, grad)

    w_grad = pl.pallas_call(
        finish_kernel,
        out_shape=jax.ShapeDtypeStruct((panel, width), F32),
        in_specs=vmem(3) + hbm(1),
        out_specs=pl.BlockSpec(memory_space=pltpu.VMEM),
        compiler_params=params(panel * width * 10),
        cost_estimate=cost(panel * width, panel * width * 10),
        name="finish",
    )(grad, received, column, *keep(emb_grad))
    return (w_grad, emb_grad)


def solution(mesh):
    in_specs = (
        P(("enc", "lab"), None),
        P("lab", None),
        P("lab"),
        P(("enc", "lab"), None),
        P(("enc", "lab"), None),
        P(("enc", "lab"), None),
        P(("enc", "lab"), None, None),
    )
    out_specs = (P("lab", None), P(("enc", "lab"), None))
    return jax.shard_map(shards, mesh=mesh, in_specs=in_specs, out_specs=out_specs, check_vma=False)
```

```python
import functools
import math

import jax
import jax.numpy as jnp
from jax import lax
from jax.experimental import pallas as pl
from jax.experimental.pallas import tpu as pltpu
from jax.sharding import PartitionSpec as P

BF16 = jnp.bfloat16
F32 = jnp.float32
LANES = 128
PACKED = 16
ROWS = 256
MIB = 1024 * 1024


def flip(value, axis, mask, odd=None):
    masks = (mask, mask if odd is None else odd)
    return lax.ppermute(value, axis, [(i, i ^ masks[i & 1]) for i in range(lax.axis_size(axis))])


def bit_groups(count):
    masks = [1 << b for b in range(1, count.bit_length() - 1)]
    return [tuple(masks[i : i + 2]) for i in range(0, len(masks), 2)]


def partners(group):
    if len(group) == 1:
        return [(group[0], group[0])]
    low, high = group
    return [(low, high), (high, low), (low | high, low | high)]


def block_masks(groups):
    masks = [(0, 0)]
    for group in groups:
        masks = [(e ^ x, o ^ y) for e, o in [(0, 0)] + partners(group) for x, y in masks]
    return masks


def fetch(sources, targets, sem):
    copies = [pltpu.make_async_copy(x, y, sem.at[i]) for i, (x, y) in enumerate(zip(sources, targets))]
    for copy in copies:
        copy.start()
    for copy in copies:
        copy.wait()


def flag_column(flags):
    panel = flags.shape[1]
    diagonal = lax.broadcasted_iota(jnp.int32, (panel, panel), 0) == lax.broadcasted_iota(
        jnp.int32, (panel, panel), 1
    )
    spread = jnp.broadcast_to(flags.astype(F32), (panel, panel))
    return jnp.sum(jnp.where(diagonal, spread, 0.0), axis=1, keepdims=True)


def pack_kernel(
    classifier_hbm, valid_hbm, short_hbm, live_hbm, pos_hbm, neg_hbm, rows_ref, column_ref, index_ref,
    classifier_ref, valid_ref, short_ref, live_ref, pos_ref, neg_ref, sem, *, scale
):
    slots, negatives, docs = neg_ref.shape
    fetch(
        (classifier_hbm, valid_hbm, short_hbm, live_hbm, pos_hbm, neg_hbm),
        (classifier_ref, valid_ref, short_ref, live_ref, pos_ref, neg_ref),
        sem,
    )
    column = flag_column(valid_ref[...])
    rows_ref[...] = (classifier_ref[...] * column).astype(BF16)
    column_ref[...] = jnp.broadcast_to(column * scale, column_ref.shape)
    index_ref[...] = jnp.concatenate(
        [
            neg_ref[...].reshape(slots * negatives, docs),
            pos_ref[...],
            jnp.where(live_ref[...] > 0, short_ref[...], -1),
        ],
        0,
    ).astype(F32).astype(BF16)


def turn_kernel(emb_hbm, other_ref, own_ref, own_turned_ref, other_turned_ref, sem):
    copy = pltpu.make_async_copy(emb_hbm, own_ref, sem)
    copy.start()
    other_turned_ref[...] = other_ref[...].T
    copy.wait()
    own_turned_ref[...] = own_ref[...].T


def targets_kernel(index_own_ref, index_other_ref, after_ref, target_own_ref, target_other_ref, *, panel, slots, masks):
    me = lax.axis_index("lab")
    docs = index_own_ref.shape[1]
    negatives = index_own_ref.shape[0] // slots - 2
    shape = (panel // PACKED, PACKED, LANES)
    label = PACKED * lax.broadcasted_iota(jnp.int32, shape, 0) + lax.broadcasted_iota(jnp.int32, shape, 1)
    label = label.astype(F32).astype(BF16)
    one, zero = jnp.ones((), BF16), jnp.zeros((), BF16)

    def fill(index_ref, out_ref, lanes):
        index = index_ref[:, lanes].astype(F32)

        def row(at):
            return jnp.broadcast_to(index[at : at + 1], (PACKED, LANES))

        values, relative = [], []
        for s in range(slots):
            count = jnp.zeros(shape, BF16)
            for k in range(negatives):
                count = count + jnp.where(row(s * negatives + k).astype(BF16)[None] == label, one, zero)
            hot = row(slots * negatives + s).astype(BF16)[None] == label
            values.append(jnp.where(hot, -one - count, count))
            relative.append(row(slots * (negatives + 1) + s).astype(jnp.int32) ^ me)
        for j, (even_mask, odd_mask) in enumerate(masks):
            mask = even_mask + (me & 1) * (odd_mask - even_mask)
            block = jnp.zeros(shape, BF16)
            for s in range(slots):
                chosen = jnp.where(relative[s] == mask, 1.0, 0.0).astype(BF16)
                block = block + chosen[None] * values[s]
            out_ref[pl.ds(j * panel, panel), lanes] = block.reshape(panel, LANES)

    def chunk(i, carry):
        lanes = pl.ds(pl.multiple_of(i * LANES, LANES), LANES)
        fill(index_own_ref, target_own_ref, lanes)
        fill(index_other_ref, target_other_ref, lanes)
        return carry

    lax.fori_loop(0, docs // LANES, chunk, 0)


def score_kernel(*refs, which, after):
    refs = list(refs)

    def take(number):
        return [refs.pop(0) for _ in range(number)]

    count = len(which)
    piece_refs, emb_refs, turned_refs, target_refs = take(count), take(2), take(2), take(2)
    take(after)
    grad_refs, dlogit_refs = take(count), [take(count) for _ in range(2)]
    each = piece_refs[0].shape[0]
    if each * count <= ROWS:
        units = [[(i, 0, each) for i in range(count)]]
    else:
        rows = min(ROWS, each)
        units = [[(i, start, rows)] for i in range(count) for start in range(0, each, rows)]

    def gather(unit, refs, at=lambda i: 0):
        values = [refs[i][at(i) + start : at(i) + start + rows] for i, start, rows in unit]
        return values[0] if len(values) == 1 else jnp.concatenate(values, 0)

    for unit in units:
        block = gather(unit, piece_refs)
        logits = [jnp.dot(block, ref[...], preferred_element_type=F32) for ref in turned_refs]
        dlogits = []
        for x, target_ref in zip(logits, target_refs):
            signed = gather(unit, [target_ref] * count, lambda i: which[i] * each).astype(F32)
            dlogits.append((signed * jax.nn.sigmoid(jnp.where(signed < 0, -x, x))).astype(BF16))
        grad = jnp.dot(
            jnp.concatenate(dlogits, 1),
            jnp.concatenate([ref[...] for ref in emb_refs], 0),
            preferred_element_type=F32,
        )
        off = 0
        for i, start, rows in unit:
            for d, out_refs in zip(dlogits, dlogit_refs):
                out_refs[i][start : start + rows] = d[off : off + rows]
            grad_refs[i][start : start + rows] = grad[off : off + rows].astype(grad_refs[i].dtype)
            off += rows
    for ref in grad_refs:
        if ref.shape[0] > each:
            ref[each:] = jnp.zeros((ref.shape[0] - each, ref.shape[1]), ref.dtype)


def join_kernel(*refs, count):
    for k in range(3):
        out_ref = refs[3 * count + k]
        at = 0
        for ref in refs[k * count : (k + 1) * count]:
            out_ref[at : at + ref.shape[0]] = ref[...]
            at += ref.shape[0]


def emb_kernel(d_own_ref, d_other_ref, c_own_ref, c_other_ref, after_ref, out_ref):
    dims = (((0,), (0,)), ((), ()))
    out_ref[...] = lax.dot_general(
        d_own_ref[...], c_own_ref[...], dims, preferred_element_type=F32
    ) + lax.dot_general(d_other_ref[...], c_other_ref[...], dims, preferred_element_type=F32)


def finish_kernel(grad_ref, received_ref, column_ref, after_hbm, out_ref):
    out_ref[...] = (grad_ref[...] + received_ref[...].astype(F32)) * column_ref[:, :1]


def hbm(count):
    return [pl.BlockSpec(memory_space=pltpu.HBM)] * count


def vmem(count):
    return [pl.BlockSpec(memory_space=pltpu.VMEM)] * count


def keep(*arrays):
    return [pltpu.with_memory_space_constraint(x, pltpu.HBM) for x in arrays]


def cost(flops, nbytes):
    return pl.CostEstimate(flops=flops, bytes_accessed=nbytes, transcendentals=0)


def params(*sizes):
    return pltpu.CompilerParams(vmem_limit_bytes=(2 * sum(sizes) // MIB + 4) * MIB)


def shards(embeddings, classifier, label_valid, shortlist, slot_live, positive, negative):
    lab = lax.axis_size("lab")
    enc = lax.axis_size("enc")
    docs, width = embeddings.shape
    panel = classifier.shape[0]
    slots = shortlist.shape[1]
    half = lab // 2 * panel
    groups = bit_groups(lab)

    negatives = negative.shape[2]
    height = slots * (negatives + 2)
    packed, column, index_own = pl.pallas_call(
        functools.partial(pack_kernel, scale=1.0 / math.sqrt(docs * enc * slots)),
        out_shape=[
            jax.ShapeDtypeStruct((panel, width), BF16),
            jax.ShapeDtypeStruct((panel, LANES), F32),
            jax.ShapeDtypeStruct((height, docs), BF16),
        ],
        in_specs=hbm(6),
        out_specs=vmem(3),
        scratch_shapes=[pltpu.VMEM((panel, width), F32), pltpu.VMEM((1, panel), jnp.int32)]
        + [pltpu.VMEM((slots, docs), jnp.int32)] * 3
        + [pltpu.VMEM((slots, negatives, docs), jnp.int32), pltpu.SemaphoreType.DMA((6,))],
        compiler_params=params(panel * width * 6, height * docs * 4),
        cost_estimate=cost(panel * width, panel * width * 6 + height * docs * 4),
        name="pack",
    )(
        *keep(
            classifier, label_valid.reshape(1, panel), shortlist.T, slot_live.T, positive.T,
            negative.transpose(1, 2, 0),
        )
    )
    pieces = [packed]
    for group in groups:
        own = pieces[0] if len(pieces) == 1 else jnp.concatenate(pieces, 0)
        pieces = [own] + [flip(own, "lab", *masks) for masks in partners(group)]

    emb_other = flip(embeddings, "lab", 1)
    index_other = flip(index_own, "lab", 1)
    emb_own, own_turned, other_turned = pl.pallas_call(
        turn_kernel,
        out_shape=[jax.ShapeDtypeStruct((docs, width), BF16)]
        + [jax.ShapeDtypeStruct((width, docs), BF16)] * 2,
        in_specs=hbm(1) + vmem(1),
        out_specs=vmem(3),
        scratch_shapes=[pltpu.SemaphoreType.DMA],
        compiler_params=params(docs * width * 10),
        cost_estimate=cost(docs * width, docs * width * 10),
        name="turn",
    )(*keep(embeddings), emb_other)
    target_own, target_other = pl.pallas_call(
        functools.partial(targets_kernel, panel=panel, slots=slots, masks=block_masks(groups)),
        out_shape=[jax.ShapeDtypeStruct((half, docs), BF16)] * 2,
        in_specs=vmem(3),
        out_specs=vmem(2),
        compiler_params=params(height * docs * 8, docs * half * 4),
        cost_estimate=cost(docs * panel * slots * 80, height * docs * 8 + docs * half * 4),
        name="targets",
    )(index_own, index_other, other_turned)

    each = pieces[0].shape[0]
    number = len(pieces)

    def score(which, after):
        count, rows = len(which), each * len(which)
        outs = pl.pallas_call(
            functools.partial(score_kernel, which=which, after=len(after)),
            out_shape=[
                jax.ShapeDtypeStruct((each + (PACKED if i == 3 else 0), width), BF16 if i else F32)
                for i in which
            ]
            + [jax.ShapeDtypeStruct((each, docs), BF16)] * (2 * count),
            in_specs=vmem(count + 6 + len(after)),
            out_specs=vmem(3 * count),
            compiler_params=params(8 * docs * width, 16 * rows * docs, 12 * rows * width),
            cost_estimate=cost(
                8 * docs * rows * width, 8 * docs * width + 8 * rows * docs + 8 * rows * width
            ),
            name="score",
        )(
            *[pieces[i] for i in which], emb_own, emb_other, own_turned, other_turned,
            target_own, target_other, *after,
        )
        return outs[:count], outs[count : 2 * count], outs[2 * count :]

    order = [number - 1, 0] + list(range(1, number - 1))
    grads, dlogits = {}, ([], [])
    for which in [w for w in (order[:2], order[2:]) if w]:
        results = score(which, list(grads.values())[:1])
        grads.update(zip(which, results[0]))
        for store, values in zip(dlogits, results[1:]):
            store += values
    classifier_own, d_own, d_theirs = pl.pallas_call(
        functools.partial(join_kernel, count=number),
        out_shape=[jax.ShapeDtypeStruct((half, width), BF16)]
        + [jax.ShapeDtypeStruct((half, docs), BF16)] * 2,
        in_specs=vmem(3 * number),
        out_specs=vmem(3),
        compiler_params=params(4 * half * width, 8 * half * docs),
        cost_estimate=cost(0, 4 * half * width + 8 * half * docs),
        name="join",
    )(*[pieces[i] for i in order], *dlogits[0], *dlogits[1])

    grad = None
    for group in reversed(groups):
        masks = partners(group)
        if grad is not None:
            grad = grad.reshape(len(masks) + 1, -1, width)
            grads = [grad[0]] + [grad[i].astype(BF16) for i in range(1, len(masks) + 1)]
        received = []
        for i in reversed(range(len(masks))):
            value = grads[i + 1]
            if i == 2 and value.shape[0] == grads[0].shape[0]:
                value = jnp.concatenate([value, value[:1]], 0)
            received.append(flip(value, "lab", *masks[i])[: grads[0].shape[0]])
        grad = grads[0]
        for r in received:
            grad = grad + r.astype(F32)
    if grad is None:
        grad = grads[0]
    d_other, classifier_other = flip(d_theirs, "lab", 1), flip(classifier_own, "lab", 1)
    bits = [1 << bit for bit in range(enc.bit_length() - 1)]
    for bit in bits[:-1]:
        grad = grad + flip(grad.astype(BF16), "enc", bit).astype(F32)
    received = flip(grad.astype(BF16), "enc", bits[-1])

    emb_grad = pl.pallas_call(
        emb_kernel,
        out_shape=jax.ShapeDtypeStruct((docs, width), F32),
        in_specs=vmem(5),
        out_specs=pl.BlockSpec(memory_space=pltpu.VMEM),
        compiler_params=params(8 * docs * width, 4 * half * docs, 4 * half * width),
        cost_estimate=cost(4 * docs * half * width, 4 * docs * width + 4 * half * docs + 4 * half * width),
        name="emb_grad",
    )(d_own, d_other, classifier_own, classifier_other, grad)

    w_grad = pl.pallas_call(
        finish_kernel,
        out_shape=jax.ShapeDtypeStruct((panel, width), F32),
        in_specs=vmem(3) + hbm(1),
        out_specs=pl.BlockSpec(memory_space=pltpu.VMEM),
        compiler_params=params(panel * width * 10),
        cost_estimate=cost(panel * width, panel * width * 10),
        name="finish",
    )(grad, received, column, *keep(emb_grad))
    return (w_grad, emb_grad)


def solution(mesh):
    in_specs = (
        P(("enc", "lab"), None),
        P("lab", None),
        P("lab"),
        P(("enc", "lab"), None),
        P(("enc", "lab"), None),
        P(("enc", "lab"), None),
        P(("enc", "lab"), None, None),
    )
    out_specs = (P("lab", None), P(("enc", "lab"), None))
    return jax.shard_map(shards, mesh=mesh, in_specs=in_specs, out_specs=out_specs, check_vma=False)
```

```python
import functools
import math

import jax
import jax.numpy as jnp
from jax import lax
from jax.experimental import pallas as pl
from jax.experimental.pallas import tpu as pltpu
from jax.sharding import PartitionSpec as P

BF16 = jnp.bfloat16
F32 = jnp.float32
LANES = 128
PACKED = 16
ROWS = 256
MIB = 1024 * 1024


def flip(value, axis, mask):
    return lax.ppermute(value, axis, [(i, i ^ mask) for i in range(lax.axis_size(axis))])


def bit_groups(count):
    masks = [1 << b for b in range(1, count.bit_length() - 1)]
    return [tuple(masks[i : i + 2]) for i in range(0, len(masks), 2)]


def group_masks(group):
    return [group[0]] if len(group) == 1 else [group[0], group[1], group[0] | group[1]]


def fetch(sources, targets, sem):
    copies = [pltpu.make_async_copy(x, y, sem.at[i]) for i, (x, y) in enumerate(zip(sources, targets))]
    for copy in copies:
        copy.start()
    for copy in copies:
        copy.wait()


def flag_column(flags):
    panel = flags.shape[1]
    diagonal = lax.broadcasted_iota(jnp.int32, (panel, panel), 0) == lax.broadcasted_iota(
        jnp.int32, (panel, panel), 1
    )
    spread = jnp.broadcast_to(flags.astype(F32), (panel, panel))
    return jnp.sum(jnp.where(diagonal, spread, 0.0), axis=1, keepdims=True)


def pack_kernel(
    classifier_hbm, valid_hbm, short_hbm, live_hbm, pos_hbm, neg_hbm, rows_ref, column_ref, index_ref,
    classifier_ref, valid_ref, short_ref, live_ref, pos_ref, neg_ref, sem, *, scale
):
    slots, negatives, docs = neg_ref.shape
    fetch(
        (classifier_hbm, valid_hbm, short_hbm, live_hbm, pos_hbm, neg_hbm),
        (classifier_ref, valid_ref, short_ref, live_ref, pos_ref, neg_ref),
        sem,
    )
    column = flag_column(valid_ref[...])
    rows_ref[...] = (classifier_ref[...] * column).astype(BF16)
    column_ref[...] = jnp.broadcast_to(column * scale, column_ref.shape)
    index_ref[...] = jnp.concatenate(
        [
            neg_ref[...].reshape(slots * negatives, docs),
            pos_ref[...],
            jnp.where(live_ref[...] > 0, short_ref[...], -1),
        ],
        0,
    ).astype(F32).astype(BF16)


def turn_kernel(emb_hbm, other_ref, own_ref, own_turned_ref, other_turned_ref, sem):
    copy = pltpu.make_async_copy(emb_hbm, own_ref, sem)
    copy.start()
    other_turned_ref[...] = other_ref[...].T
    copy.wait()
    own_turned_ref[...] = own_ref[...].T


def targets_kernel(index_own_ref, index_other_ref, after_ref, target_own_ref, target_other_ref, *, panel, slots):
    me = lax.axis_index("lab")
    docs = index_own_ref.shape[1]
    negatives = index_own_ref.shape[0] // slots - 2
    shape = (panel // PACKED, PACKED, LANES)
    label = PACKED * lax.broadcasted_iota(jnp.int32, shape, 0) + lax.broadcasted_iota(jnp.int32, shape, 1)
    label = label.astype(F32).astype(BF16)
    one, zero = jnp.ones((), BF16), jnp.zeros((), BF16)

    def fill(index_ref, out_ref, lanes):
        index = index_ref[:, lanes].astype(F32)

        def row(at):
            return jnp.broadcast_to(index[at : at + 1], (PACKED, LANES))

        values, relative = [], []
        for s in range(slots):
            count = jnp.zeros(shape, BF16)
            for k in range(negatives):
                count = count + jnp.where(row(s * negatives + k).astype(BF16)[None] == label, one, zero)
            hot = row(slots * negatives + s).astype(BF16)[None] == label
            values.append(jnp.where(hot, -one - count, count))
            relative.append(row(slots * (negatives + 1) + s).astype(jnp.int32) ^ me)
        for j in range(out_ref.shape[0] // panel):
            block = jnp.zeros(shape, BF16)
            for s in range(slots):
                chosen = jnp.where(relative[s] == 2 * j, 1.0, 0.0).astype(BF16)
                block = block + chosen[None] * values[s]
            out_ref[pl.ds(j * panel, panel), lanes] = block.reshape(panel, LANES)

    def chunk(i, carry):
        lanes = pl.ds(pl.multiple_of(i * LANES, LANES), LANES)
        fill(index_own_ref, target_own_ref, lanes)
        fill(index_other_ref, target_other_ref, lanes)
        return carry

    lax.fori_loop(0, docs // LANES, chunk, 0)


def score_kernel(*refs, which, after):
    refs = list(refs)

    def take(number):
        return [refs.pop(0) for _ in range(number)]

    count = len(which)
    piece_refs, emb_refs, turned_refs, target_refs = take(count), take(2), take(2), take(2)
    take(after)
    grad_refs, dlogit_refs = take(count), [take(count) for _ in range(2)]
    each = piece_refs[0].shape[0]
    if each * count <= ROWS:
        units = [[(i, 0, each) for i in range(count)]]
    else:
        rows = min(ROWS, each)
        units = [[(i, start, rows)] for i in range(count) for start in range(0, each, rows)]

    def gather(unit, refs, at=lambda i: 0):
        values = [refs[i][at(i) + start : at(i) + start + rows] for i, start, rows in unit]
        return values[0] if len(values) == 1 else jnp.concatenate(values, 0)

    for unit in units:
        block = gather(unit, piece_refs)
        both = jnp.concatenate([ref[...] for ref in turned_refs], 1)
        logits = jnp.split(jnp.dot(block, both, preferred_element_type=F32), 2, 1)
        dlogits = []
        for x, target_ref in zip(logits, target_refs):
            signed = gather(unit, [target_ref] * count, lambda i: which[i] * each).astype(F32)
            dlogits.append((signed * jax.nn.sigmoid(jnp.where(signed < 0, -x, x))).astype(BF16))
        joined = jnp.concatenate(dlogits, 1)
        grad = jnp.concatenate(
            [
                jnp.dot(
                    joined,
                    jnp.concatenate([ref[:, n : n + 256] for ref in emb_refs], 0),
                    preferred_element_type=F32,
                )
                for n in range(0, emb_refs[0].shape[1], 256)
            ],
            1,
        )
        off = 0
        for i, start, rows in unit:
            for d, out_refs in zip(dlogits, dlogit_refs):
                out_refs[i][start : start + rows] = d[off : off + rows]
            grad_refs[i][start : start + rows] = grad[off : off + rows].astype(grad_refs[i].dtype)
            off += rows


def join_kernel(*refs, count):
    for k in range(3):
        out_ref = refs[3 * count + k]
        at = 0
        for ref in refs[k * count : (k + 1) * count]:
            out_ref[at : at + ref.shape[0]] = ref[...]
            at += ref.shape[0]


def emb_kernel(d_own_ref, d_other_ref, c_own_ref, c_other_ref, after_ref, out_ref):
    dims = (((0,), (0,)), ((), ()))
    out_ref[...] = lax.dot_general(
        d_own_ref[...], c_own_ref[...], dims, preferred_element_type=F32
    ) + lax.dot_general(d_other_ref[...], c_other_ref[...], dims, preferred_element_type=F32)


def finish_kernel(grad_ref, received_ref, column_ref, after_hbm, out_ref):
    out_ref[...] = (grad_ref[...] + received_ref[...].astype(F32)) * column_ref[:, :1]


def hbm(count):
    return [pl.BlockSpec(memory_space=pltpu.HBM)] * count


def vmem(count):
    return [pl.BlockSpec(memory_space=pltpu.VMEM)] * count


def keep(*arrays):
    return [pltpu.with_memory_space_constraint(x, pltpu.HBM) for x in arrays]


def cost(flops, nbytes):
    return pl.CostEstimate(flops=flops, bytes_accessed=nbytes, transcendentals=0)


def params(*sizes):
    return pltpu.CompilerParams(vmem_limit_bytes=(2 * sum(sizes) // MIB + 4) * MIB)


def shards(embeddings, classifier, label_valid, shortlist, slot_live, positive, negative):
    lab = lax.axis_size("lab")
    enc = lax.axis_size("enc")
    docs, width = embeddings.shape
    panel = classifier.shape[0]
    slots = shortlist.shape[1]
    half = lab // 2 * panel
    groups = bit_groups(lab)

    negatives = negative.shape[2]
    height = slots * (negatives + 2)
    packed, column, index_own = pl.pallas_call(
        functools.partial(pack_kernel, scale=1.0 / math.sqrt(docs * enc * slots)),
        out_shape=[
            jax.ShapeDtypeStruct((panel, width), BF16),
            jax.ShapeDtypeStruct((panel, LANES), F32),
            jax.ShapeDtypeStruct((height, docs), BF16),
        ],
        in_specs=hbm(6),
        out_specs=vmem(3),
        scratch_shapes=[pltpu.VMEM((panel, width), F32), pltpu.VMEM((1, panel), jnp.int32)]
        + [pltpu.VMEM((slots, docs), jnp.int32)] * 3
        + [pltpu.VMEM((slots, negatives, docs), jnp.int32), pltpu.SemaphoreType.DMA((6,))],
        compiler_params=params(panel * width * 6, height * docs * 4),
        cost_estimate=cost(panel * width, panel * width * 6 + height * docs * 4),
        name="pack",
    )(
        *keep(
            classifier, label_valid.reshape(1, panel), shortlist.T, slot_live.T, positive.T,
            negative.transpose(1, 2, 0),
        )
    )
    pieces = [packed]
    for group in groups:
        own = pieces[0] if len(pieces) == 1 else jnp.concatenate(pieces, 0)
        pieces = [own] + [flip(own, "lab", mask) for mask in group_masks(group)]

    emb_other = flip(embeddings, "lab", 1)
    index_other = flip(index_own, "lab", 1)
    emb_own, own_turned, other_turned = pl.pallas_call(
        turn_kernel,
        out_shape=[jax.ShapeDtypeStruct((docs, width), BF16)]
        + [jax.ShapeDtypeStruct((width, docs), BF16)] * 2,
        in_specs=hbm(1) + vmem(1),
        out_specs=vmem(3),
        scratch_shapes=[pltpu.SemaphoreType.DMA],
        compiler_params=params(docs * width * 10),
        cost_estimate=cost(docs * width, docs * width * 10),
        name="turn",
    )(*keep(embeddings), emb_other)
    target_own, target_other = pl.pallas_call(
        functools.partial(targets_kernel, panel=panel, slots=slots),
        out_shape=[jax.ShapeDtypeStruct((half, docs), BF16)] * 2,
        in_specs=vmem(3),
        out_specs=vmem(2),
        compiler_params=params(height * docs * 8, docs * half * 4),
        cost_estimate=cost(docs * panel * slots * 80, height * docs * 8 + docs * half * 4),
        name="targets",
    )(index_own, index_other, other_turned)

    each = pieces[0].shape[0]
    number = len(pieces)

    def score(which, after):
        count, rows = len(which), each * len(which)
        outs = pl.pallas_call(
            functools.partial(score_kernel, which=which, after=len(after)),
            out_shape=[jax.ShapeDtypeStruct((each, width), BF16 if i else F32) for i in which]
            + [jax.ShapeDtypeStruct((each, docs), BF16)] * (2 * count),
            in_specs=vmem(count + 6 + len(after)),
            out_specs=vmem(3 * count),
            compiler_params=params(8 * docs * width, 16 * rows * docs, 12 * rows * width),
            cost_estimate=cost(
                8 * docs * rows * width, 8 * docs * width + 8 * rows * docs + 8 * rows * width
            ),
            name="score",
        )(
            *[pieces[i] for i in which], emb_own, emb_other, own_turned, other_turned,
            target_own, target_other, *after,
        )
        return outs[:count], outs[count : 2 * count], outs[2 * count :]

    order = [number - 1, 0] + list(range(1, number - 1))
    grads, dlogits = {}, ([], [])
    for which in [w for w in (order[:2], order[2:]) if w]:
        results = score(which, list(grads.values())[:1])
        grads.update(zip(which, results[0]))
        for store, values in zip(dlogits, results[1:]):
            store += values
    classifier_own, d_own, d_theirs = pl.pallas_call(
        functools.partial(join_kernel, count=number),
        out_shape=[jax.ShapeDtypeStruct((half, width), BF16)]
        + [jax.ShapeDtypeStruct((half, docs), BF16)] * 2,
        in_specs=vmem(3 * number),
        out_specs=vmem(3),
        compiler_params=params(4 * half * width, 8 * half * docs),
        cost_estimate=cost(0, 4 * half * width + 8 * half * docs),
        name="join",
    )(*[pieces[i] for i in order], *dlogits[0], *dlogits[1])

    grad = None
    for group in reversed(groups):
        masks = group_masks(group)
        if grad is not None:
            grad = grad.reshape(len(masks) + 1, -1, width)
            grads = [grad[0]] + [grad[i].astype(BF16) for i in range(1, len(masks) + 1)]
        received = []
        for i in reversed(range(len(masks))):
            value = grads[i + 1]
            if i == 2:
                value = jnp.concatenate([value, value[:1]], 0)
            received.append(flip(value, "lab", masks[i])[: grads[i + 1].shape[0]])
        grad = grads[0]
        for r in received:
            grad = grad + r.astype(F32)
    if grad is None:
        grad = grads[0]
    d_other, classifier_other = flip(d_theirs, "lab", 1), flip(classifier_own, "lab", 1)
    bits = [1 << bit for bit in range(enc.bit_length() - 1)]
    for bit in bits[:-1]:
        grad = grad + flip(grad.astype(BF16), "enc", bit).astype(F32)
    received = flip(grad.astype(BF16), "enc", bits[-1])

    emb_grad = pl.pallas_call(
        emb_kernel,
        out_shape=jax.ShapeDtypeStruct((docs, width), F32),
        in_specs=vmem(5),
        out_specs=pl.BlockSpec(memory_space=pltpu.VMEM),
        compiler_params=params(8 * docs * width, 4 * half * docs, 4 * half * width),
        cost_estimate=cost(4 * docs * half * width, 4 * docs * width + 4 * half * docs + 4 * half * width),
        name="emb_grad",
    )(d_own, d_other, classifier_own, classifier_other, grad)

    w_grad = pl.pallas_call(
        finish_kernel,
        out_shape=jax.ShapeDtypeStruct((panel, width), F32),
        in_specs=vmem(3) + hbm(1),
        out_specs=pl.BlockSpec(memory_space=pltpu.VMEM),
        compiler_params=params(panel * width * 10),
        cost_estimate=cost(panel * width, panel * width * 10),
        name="finish",
    )(grad, received, column, *keep(emb_grad))
    return (w_grad, emb_grad)


def solution(mesh):
    in_specs = (
        P(("enc", "lab"), None),
        P("lab", None),
        P("lab"),
        P(("enc", "lab"), None),
        P(("enc", "lab"), None),
        P(("enc", "lab"), None),
        P(("enc", "lab"), None, None),
    )
    out_specs = (P("lab", None), P(("enc", "lab"), None))
    return jax.shard_map(shards, mesh=mesh, in_specs=in_specs, out_specs=out_specs, check_vma=False)
```
